32 devices in a mesh: row: 4 (over y, x), col: 8 (over z, core).
Axes of the slice: x: 2, y: 2, z: 4, core: 2. Of those that a mesh axis runs over, the one named last changes fastest.
Arguments:
- a_tiles: bfloat16 [3072, 3200], P(('row', 'col')), may hold values from -4 to 4
- a_owner: int32 [3072], P(('row', 'col')), may hold values from 0 to 31, as said below
- a_offset: int32 [3072, 2], P(('row', 'col')), may hold values from 0 to 560, as said below
- b_tiles: bfloat16 [3072, 3200], P(('row', 'col')), may hold values from -6 to 6
- b_owner: int32 [3072], P(('row', 'col')), may hold values from 0 to 31, as said below
- b_offset: int32 [3072, 2], P(('row', 'col')), may hold values from 0 to 560, as said below
- patch_valid: int32 [48, 128], P('row', 'col'), may hold values 0 or 1
Outputs:
- flow_field: float32 [2, 48, 128], P(None, 'row', 'col')
- mesh_field: float32 [2, 48, 128], P(None, 'row', 'col')
The draws below stay inside these ranges and needn't reach their ends.
Inputs may be any that keep to these rules, and one draw needn't show every extreme that they name: `a_owner`: each region owner receives exactly 96 first-section tiles, one for every tile position of its region; a device sends either no tile or exactly 4 tiles to one owner. `a_offset`: row offsets are multiples of 40 below 480, column offsets multiples of 80 below 640; each owner's tiles cover its region exactly once. `b_owner`: each region owner receives exactly 96 next-section tiles, one for every tile position of its region; a device sends either no tile or exactly 4 tiles to one owner. `b_offset`: row offsets are multiples of 40 below 480, column offsets multiples of 80 below 640; each owner's tiles cover its region exactly once.
All inputs are finite; a program needn't handle non-finite values. No bound on the sum of `patch_valid` on one device may be relied on, other than what follows from the above.
Results may differ from the reference program's by a relative error of at most 0.004.
Values may be sent and summed in bfloat16 or wider, within the bound.
A program may use at most 64 MiB of HBM per device.

```python
import math
import jax
import jax.numpy as jnp
from jax import lax

PATCH = 160
STRIDE = 40
TY = 12
TX = 8
SWEEPS = 3
MARGIN = 60
RH = 480
RW = 640
TH = 40
TW = 80
TPR = 96
CAP = 4
NGH = 48
NGW = 128
SH = 1920
SW = 5120
NTILES = 3072


def routing(key, salt):
    salted = jax.random.fold_in(key, salt)
    subkeys = jax.random.split(salted, 5)
    devices = NTILES // TPR
    owners_each = TPR // CAP
    offset_set = jax.random.permutation(subkeys[0], devices)[:owners_each]
    sender_rank = jax.random.permutation(subkeys[1], devices)
    owner_label = jax.random.permutation(subkeys[2], devices)
    tile_perm = jax.vmap(lambda sub: jax.random.permutation(sub, TPR))(jax.random.split(subkeys[3], devices))
    place_perm = jax.vmap(lambda sub: jax.random.permutation(sub, TPR))(jax.random.split(subkeys[4], devices))
    group_index = tile_perm // CAP
    slot_index = tile_perm % CAP
    tile_owner = owner_label[(sender_rank[:, None] + offset_set[group_index]) % devices]
    position = place_perm[tile_owner, group_index * CAP + slot_index]
    row_offset = position // TX * TH
    col_offset = position % TX * TW
    offsets = jnp.stack([row_offset, col_offset], axis=-1)
    return (tile_owner.reshape(-1).astype(jnp.int32), offsets.reshape(-1, 2).astype(jnp.int32))


def textures(key):
    salted = jax.random.fold_in(key, 11)
    subkeys = jax.random.split(salted, 3)
    shifts = jax.random.randint(subkeys[2], (SH // RH, SW // RW, 2), -STRIDE, STRIDE + 1)
    texture = jax.random.truncated_normal(subkeys[0], -4.0, 4.0, (SH, SW), jnp.float32)
    noise_field = jax.random.truncated_normal(subkeys[1], -4.0, 4.0, (SH, SW), jnp.float32)
    pixel_rows = jnp.arange(SH, dtype=jnp.int32)
    pixel_cols = jnp.arange(SW, dtype=jnp.int32)
    region_row = (pixel_rows // RH)[:, None]
    region_col = (pixel_cols // RW)[None, :]
    shift_y = shifts[:, :, 0][region_row, region_col]
    shift_x = shifts[:, :, 1][region_row, region_col]
    source_y = jnp.clip(pixel_rows[:, None] - shift_y, 0, SH - 1)
    source_x = jnp.clip(pixel_cols[None, :] - shift_x, 0, SW - 1)
    section_one = texture
    section_two = texture[source_y, source_x] + 0.5 * noise_field
    return (section_one, section_two)


def cut_tiles(slab, tile_owner, tile_offset):
    region_cols = SW // RW
    block_row = tile_owner // region_cols * TY + tile_offset[:, 0] // TH
    block_col = tile_owner % region_cols * TX + tile_offset[:, 1] // TW
    blocks = slab.reshape(SH // TH, TH, SW // TW, TW).transpose(0, 2, 1, 3)
    return blocks[block_row, block_col].reshape(-1, TH * TW)


def draw_a_owner(key, part):
    return routing(key, 1)[0]


def draw_a_offset(key, part):
    return routing(key, 1)[1]


def draw_b_owner(key, part):
    return routing(key, 2)[0]


def draw_b_offset(key, part):
    return routing(key, 2)[1]


def draw_a_tiles(key, part):
    tile_owner, tile_offset = routing(key, 1)
    section_one, section_two = textures(key)
    return cut_tiles(section_one, tile_owner, tile_offset).astype(jnp.bfloat16)


def draw_b_tiles(key, part):
    tile_owner, tile_offset = routing(key, 2)
    section_one, section_two = textures(key)
    return cut_tiles(section_two, tile_owner, tile_offset).astype(jnp.bfloat16)


def touch_ends(values, own_key, least, top_value):
    index_at = [jax.random.randint(jax.random.fold_in(own_key, axis), (), 0, length) for axis, length in enumerate(values.shape)]
    widest = values.shape.index(max(values.shape))
    next_to = index_at[:widest] + [(index_at[widest] + 1) % values.shape[widest]] + index_at[widest + 1:]
    return values.at[tuple(index_at)].set(least).at[tuple(next_to)].set(top_value)


def setup_inputs(seed: int = 0) -> dict:
    key_list = jax.random.split(jax.random.key(seed), 8)
    return {
        "a_tiles": draw_a_tiles(jax.random.fold_in(key_list[7], 71), 0),
        "a_owner": draw_a_owner(jax.random.fold_in(key_list[7], 71), 0),
        "a_offset": draw_a_offset(jax.random.fold_in(key_list[7], 71), 0),
        "b_tiles": draw_b_tiles(jax.random.fold_in(key_list[7], 71), 0),
        "b_owner": draw_b_owner(jax.random.fold_in(key_list[7], 71), 0),
        "b_offset": draw_b_offset(jax.random.fold_in(key_list[7], 71), 0),
        "patch_valid": touch_ends((jax.random.randint(key_list[6], (NGH, NGW), 0, 4) < 3).astype(jnp.int32), jax.random.fold_in(key_list[6], 1), 0, 1),
    }


stiffness = 1.0
tiny = 1e-06

def dft_tables():
    freq_index = jnp.arange(PATCH, dtype=jnp.int32)
    phase = (freq_index[:, None] * freq_index[None, :] % PATCH).astype(jnp.float32) * (2.0 * math.pi / PATCH)
    return (jnp.cos(phase).astype(jnp.bfloat16), jnp.sin(phase).astype(jnp.bfloat16))

def rounded(values):
    return lax.optimization_barrier(values.astype(jnp.bfloat16)).astype(jnp.float32)

def product(form, left_side, right_side):
    return jnp.einsum(form, left_side.astype(jnp.float32), right_side.astype(jnp.float32), precision=lax.Precision.HIGHEST)

def forward(patches, cosine_table, sine_table):
    right_side = jnp.concatenate([cosine_table, sine_table], axis=1)
    first_segment = rounded(product('nyx,xk->nyk', patches, right_side))
    halves = first_segment.reshape(first_segment.shape[0], PATCH, 2, PATCH)
    left_real = jnp.stack([cosine_table, -sine_table])
    left_imag = jnp.stack([-sine_table, -cosine_table])
    return (product('hky,nyhj->nkj', left_real, halves), product('hky,nyhj->nkj', left_imag, halves))

def inverse(cross_real, cross_imag, cosine_table, sine_table):
    stacked = jnp.stack([cross_real, cross_imag], axis=2)
    right_u = jnp.stack([cosine_table, -sine_table])
    right_v = jnp.stack([sine_table, cosine_table])
    inverse_u = rounded(product('nyhx,hxk->nyk', stacked, right_u))
    inverse_v = rounded(product('nyhx,hxk->nyk', stacked, right_v))
    stacked_uv = jnp.stack([inverse_u, inverse_v], axis=2)
    left_real = jnp.stack([cosine_table, -sine_table])
    return product('hky,nyhj->nkj', left_real, stacked_uv)

def patch_norm(patches):
    values = patches.astype(jnp.float32)
    return PATCH * jnp.sqrt(lax.optimization_barrier(jnp.mean(values * values, axis=(1, 2))) + tiny)

def correlate(patch_a, patch_b, cosine_table, sine_table):
    real_a, imag_a = forward(patch_a, cosine_table, sine_table)
    real_b, imag_b = forward(patch_b, cosine_table, sine_table)
    inv_norms = (1.0 / (patch_norm(patch_a) * patch_norm(patch_b)))[:, None, None]
    cross_real = rounded((real_a * real_b + imag_a * imag_b) * inv_norms)
    cross_imag = rounded((real_a * imag_b - imag_a * real_b) * inv_norms)
    correlation = inverse(cross_real, cross_imag, cosine_table, sine_table) / (PATCH * PATCH)
    weight = correlation * correlation
    weight_sum = lax.optimization_barrier(jnp.sum(weight, axis=(1, 2)))
    freq_index = jnp.arange(PATCH, dtype=jnp.int32)
    shift_units = jnp.where(freq_index < PATCH // 2, freq_index, freq_index - PATCH).astype(jnp.float32) * (16.0 / PATCH)
    flow_y = lax.optimization_barrier(jnp.sum(weight * shift_units[None, :, None], axis=(1, 2))) / (1.0 + weight_sum)
    flow_x = lax.optimization_barrier(jnp.sum(weight * shift_units[None, None, :], axis=(1, 2))) / (1.0 + weight_sum)
    return (flow_y, flow_x, weight_sum / (1.0 + weight_sum))

def assemble(tiles, tile_owner, tile_offset):
    region_cols = SW // RW
    block_row = tile_owner // region_cols * TY + tile_offset[:, 0] // TH
    block_col = tile_owner % region_cols * TX + tile_offset[:, 1] // TW
    blocks = jnp.zeros((SH // TH, SW // TW, TH * TW), tiles.dtype).at[block_row, block_col].set(tiles)
    return blocks.reshape(SH // TH, SW // TW, TH, TW).transpose(0, 2, 1, 3).reshape(SH, SW)

def reference(a_tiles, a_owner, a_offset, b_tiles, b_owner, b_offset, patch_valid):
    cosine_table, sine_table = dft_tables()
    images = jnp.stack([assemble(a_tiles, a_owner, a_offset), assemble(b_tiles, b_owner, b_offset)])
    padded = jnp.pad(images, ((0, 0), (MARGIN, MARGIN), (MARGIN, MARGIN)))

    def one_row(grid_row):
        band_strip = lax.dynamic_slice(padded, (grid_row * 0, grid_row * STRIDE, grid_row * 0), (2, PATCH, padded.shape[2]))
        pieces = [band_strip[:, :, column_step * STRIDE:column_step * STRIDE + NGW * STRIDE] for column_step in range(4)]
        windows = jnp.stack(pieces, 0).reshape(4, 2, PATCH, NGW, STRIDE).transpose(1, 3, 2, 0, 4).reshape(2, NGW, PATCH, PATCH)
        return correlate(windows[0], windows[1], cosine_table, sine_table)
    flow_y, flow_x, confidence = lax.map(one_row, jnp.arange(NGH, dtype=jnp.int32))
    flow_field = jnp.stack([flow_y, flow_x])
    valid_float = patch_valid.astype(jnp.float32)
    strength = valid_float * confidence
    data_pull = strength[None] * flow_field
    mesh_field = valid_float[None] * flow_field
    for sweep_index in range(SWEEPS):
        padded_mesh = jnp.pad(mesh_field, ((0, 0), (1, 1), (1, 1)))
        beside_all = padded_mesh[:, :-2, 1:-1] + padded_mesh[:, 2:, 1:-1] + padded_mesh[:, 1:-1, :-2] + padded_mesh[:, 1:-1, 2:]
        mesh_field = (data_pull + stiffness * beside_all) / (strength[None] + 4.0 * stiffness)
    return (flow_field, mesh_field)
```

```python
import math

import jax
import jax.numpy as jnp
import ml_dtypes
import numpy as np
from jax import lax
from jax.experimental import pallas as pl
from jax.experimental.pallas import tpu as pltpu
from jax.sharding import PartitionSpec as P

PATCH = 160
STRIDE = 40
TY = 12
TX = 8
SWEEPS = 3
MARGIN = 60


stiffness = 1.0
tiny = 1e-06


def extended_2(block, sides, width):
    for axis, dim in sides:
        count = lax.axis_size(axis)
        forward = [(i, i + 1) for i in range(count - 1)]
        backward = [(target, source) for source, target in forward]
        low = lax.ppermute(
            lax.slice_in_dim(block, block.shape[dim] - width, None, axis=dim), axis, forward
        )
        high = lax.ppermute(lax.slice_in_dim(block, 0, width, axis=dim), axis, backward)
        block = jnp.concatenate([low, block, high], axis=dim)
    return block


HALF = PATCH // 2 + 1
KPAD = 88
ROWS = 608
COLS = 768
WIN = 208


def tables():
    index = np.arange(PATCH, dtype=np.int64)
    phase = (index[:, None] * index[None, :] % PATCH).astype(np.float32) * np.float32(
        2.0 * math.pi / PATCH
    )
    cos = np.cos(phase).astype(ml_dtypes.bfloat16).astype(np.float32)
    sin = np.sin(phase).astype(ml_dtypes.bfloat16).astype(np.float32)
    sin[(index[:, None] * index[None, :]) % 80 == 0] = 0.0
    first = np.zeros((2, 416, 256), np.float32)
    for parity in range(2):
        top = 128 + 8 * parity
        first[parity, top : top + PATCH, :HALF] = cos[:, :HALF]
        first[parity, top : top + PATCH, 128 : 128 + HALF] = sin[:, :HALF]
    second = np.zeros((4 * KPAD, WIN), np.float32)
    for parity in range(2):
        left = STRIDE * parity
        top = 2 * KPAD * parity
        second[top : top + HALF, left : left + PATCH] = cos[:HALF]
        second[top + KPAD : top + KPAD + HALF, left : left + PATCH] = sin[:HALF]
    once = np.ones(HALF, np.float32)
    once[0] = once[-1] = 0.5
    third = np.zeros((PATCH, 2 * KPAD), np.float32)
    third[:, :HALF] = cos[:, :HALF] * once
    third[:, KPAD : KPAD + HALF] = sin[:, :HALF]
    fourth = np.zeros((256, 256), np.float32)
    fourth[:HALF, :PATCH] = cos[:HALF] * (2.0 * once)[:, None]
    fourth[128 : 128 + HALF, :PATCH] = -2.0 * sin[:HALF]
    band_rows = np.zeros((16, ROWS), np.float32)
    for i in range(12):
        band_rows[i, STRIDE * i : STRIDE * i + PATCH] = 1.0
    band_cols = np.zeros((COLS, 128), np.float32)
    for j in range(16):
        band_cols[STRIDE * j : STRIDE * j + PATCH, j] = 1.0
    as_bf16 = [jnp.asarray(t, jnp.bfloat16) for t in (first, second, third, fourth, band_rows)]
    return (*as_bf16, jnp.asarray(band_cols, jnp.float32))


def dot(left, right):
    return jnp.dot(left, right, preferred_element_type=jnp.float32)


def correlate_kernel(
    images, first, second, third, fourth, band_rows, band_cols, out, spec, scale, parts
):
    grid_rows, grid_cols = out.shape[1], out.shape[2]
    half_rows = ROWS // 2

    def first_part(step, carry):
        section = step // 2
        top = pl.multiple_of(step % 2 * half_rows, 16)
        for j in range(grid_cols):
            left = STRIDE * j // 128 * 128
            inside = STRIDE * j - left
            width = 256 if inside + PATCH <= 256 else 384
            parity = inside // 8 % 2
            base = 128 + 8 * parity - inside
            strip = images[section, pl.ds(top, half_rows), left : left + width]
            spec[section, pl.ds(top, half_rows), 256 * j : 256 * (j + 1)] = dot(
                strip, first[parity, base : base + width, :]
            ).astype(jnp.bfloat16)
        return carry

    lax.fori_loop(0, 4, first_part, 0)

    norms = []
    for section in range(2):
        values = images[section].astype(jnp.float32)
        squares = values * values
        high = squares.astype(jnp.bfloat16)
        low = (squares - high.astype(jnp.float32)).astype(jnp.bfloat16)
        by_rows = dot(band_rows[...], high) + dot(band_rows[...], low)
        total = jnp.dot(
            by_rows,
            band_cols[...],
            preferred_element_type=jnp.float32,
            precision=lax.Precision.HIGHEST,
        )
        norms.append(PATCH * jnp.sqrt(total / (PATCH * PATCH) + tiny))
    inv_norms = 1.0 / (norms[0] * norms[1])
    scale[...] = (inv_norms * (1.0 / (PATCH * PATCH))) * (inv_norms * (1.0 / (PATCH * PATCH)))

    lane = lax.broadcasted_iota(jnp.int32, (8, 256), 1)
    sublane = lax.broadcasted_iota(jnp.int32, (8, 256), 0)
    unit = 16.0 / PATCH
    shift_x = jnp.where(lane < PATCH // 2, lane, lane - PATCH).astype(jnp.float32) * unit
    shift_x = jnp.where(lane < PATCH, shift_x, 0.0)
    shift_y = (sublane + PATCH // 2).astype(jnp.float32) * unit

    def patch(spec_a, spec_b):
        def combos(s):
            a, e = s[:KPAD, :128], s[:KPAD, 128:]
            d, b = s[KPAD:, :128], s[KPAD:, 128:]
            return a - b, d + e, a + b, e - d

        ra, ia, ra_m, ia_m = combos(spec_a)
        rb, ib, rb_m, ib_m = combos(spec_b)
        real, imag = ra * rb + ia * ib, ia * rb - ra * ib
        real_m, imag_m = ra_m * rb_m + ia_m * ib_m, ia_m * rb_m - ra_m * ib_m
        upper = jnp.concatenate([real + real_m, imag + imag_m], axis=1)
        lower = jnp.concatenate([imag_m - imag, real - real_m], axis=1)
        cross = jnp.concatenate([upper, lower], axis=0).astype(jnp.bfloat16)
        inverse = dot(third[...], cross).astype(jnp.bfloat16)
        corr = dot(inverse, fourth[...])
        sum_0 = jnp.zeros((8, 256), jnp.float32)
        sum_1 = jnp.zeros((8, 256), jnp.float32)
        for block in range(PATCH // 8):
            top = (block * 8 + PATCH // 2) % PATCH
            piece = corr[top : top + 8]
            sum_0 = sum_0 + piece * piece
            sum_1 = sum_1 + sum_0
        results = []
        for part in (sum_0, shift_y * sum_0 - (8.0 * unit) * sum_1, shift_x * sum_0):
            part = part[:, :128] + part[:, 128:]
            results.append(jnp.sum(part, axis=0, keepdims=True))
        return results

    def pair_row(p, carry):
        top = pl.multiple_of(p * (2 * STRIDE), 16)

        def column(j, carry):
            left = pl.multiple_of(j * 256, 256)
            both = [
                dot(second[...], spec[section, pl.ds(top, WIN), pl.ds(left, 256)])
                for section in range(2)
            ]
            for parity in range(2):
                rows = slice(2 * KPAD * parity, 2 * KPAD * (parity + 1))
                for c, row in enumerate(patch(both[0][rows], both[1][rows])):
                    parts[c, parity, pl.ds(j, 1), :] = row
            return carry

        lax.fori_loop(0, grid_cols, column, 0, unroll=UNROLL)
        ones = jnp.ones((8, 128), jnp.float32)
        for parity in range(2):
            i = 2 * p + parity
            sums = [
                lax.dot_general(
                    ones,
                    parts[c, parity],
                    (((1,), (1,)), ((), ())),
                    preferred_element_type=jnp.float32,
                    precision=lax.Precision.HIGHEST,
                )[:1]
                * scale[pl.ds(i, 1), :grid_cols]
                for c in range(3)
            ]
            below = 1.0 + sums[0]
            out[0, pl.ds(i, 1), :] = sums[0] / below
            out[1, pl.ds(i, 1), :] = sums[1] / below
            out[2, pl.ds(i, 1), :] = sums[2] / below
        return carry

    lax.fori_loop(0, grid_rows // 2, pair_row, 0)


UNROLL = 1


def correlate(images, grid_rows, grid_cols):
    vmem = pl.BlockSpec(memory_space=pltpu.VMEM)
    return pl.pallas_call(
        correlate_kernel,
        out_shape=jax.ShapeDtypeStruct((3, grid_rows, grid_cols), jnp.float32),
        in_specs=[vmem] * 7,
        out_specs=vmem,
        scratch_shapes=[
            pltpu.VMEM((2, ROWS, 256 * grid_cols), jnp.bfloat16),
            pltpu.VMEM((16, 128), jnp.float32),
            pltpu.VMEM((3, 2, grid_cols, 128), jnp.float32),
        ],
        compiler_params=pltpu.CompilerParams(vmem_limit_bytes=48 * 1024 * 1024),
    )(images, *tables())


def outgoing(tiles, tile_owner, tile_offset, slot_count, capacity, tile_h, tile_w):
    tile_count = tiles.shape[0]
    tile_index = jnp.arange(tile_count, dtype=jnp.int32)
    matches = (tile_owner[:, None] == tile_owner[None, :]) & (
        tile_index[:, None] > tile_index[None, :]
    )
    earlier_count = jnp.sum(matches.astype(jnp.int32), axis=1)
    target = tile_owner * capacity + earlier_count
    select = (jnp.arange(slot_count, dtype=jnp.int32)[:, None] == target[None, :]).astype(
        jnp.bfloat16
    )
    position = tile_offset[:, 0] // tile_h * TX + tile_offset[:, 1] // tile_w + 1
    sent_tiles = jnp.dot(select, tiles, preferred_element_type=jnp.float32).astype(jnp.bfloat16)
    slot_code = jnp.dot(
        select, position.astype(jnp.bfloat16)[:, None], preferred_element_type=jnp.float32
    ).astype(jnp.bfloat16)
    return (sent_tiles, slot_code)


def incoming(received, slot_code, tile_count, tile_h, tile_w):
    wanted = jnp.arange(1, tile_count + 1, dtype=jnp.int32).astype(jnp.float32)
    select = (slot_code[:, 0].astype(jnp.float32)[None, :] == wanted[:, None]).astype(jnp.bfloat16)
    blocks = jnp.dot(select, received, preferred_element_type=jnp.float32).astype(jnp.bfloat16)
    return (
        blocks.reshape(TY, TX, tile_h, tile_w)
        .transpose(0, 2, 1, 3)
        .reshape(TY * tile_h, TX * tile_w)
    )


def route(send_a, code_a, send_b, code_b, row_count, col_count, capacity):
    devices = row_count * col_count
    tile_size = send_a.shape[1]
    code_width = code_a.shape[1]
    recv_a, got_a, recv_b, got_b = (
        lax.all_to_all(
            send_a.reshape(devices, capacity, tile_size),
            ("row", "col"),
            split_axis=0,
            concat_axis=0,
            tiled=True,
        ),
        lax.all_to_all(
            code_a.reshape(devices, capacity, code_width),
            ("row", "col"),
            split_axis=0,
            concat_axis=0,
            tiled=True,
        ),
        lax.all_to_all(
            send_b.reshape(devices, capacity, tile_size),
            ("row", "col"),
            split_axis=0,
            concat_axis=0,
            tiled=True,
        ),
        lax.all_to_all(
            code_b.reshape(devices, capacity, code_width),
            ("row", "col"),
            split_axis=0,
            concat_axis=0,
            tiled=True,
        ),
    )
    slot_count = devices * capacity
    return (
        recv_a.reshape(slot_count, tile_size),
        got_a.reshape(slot_count, code_width),
        recv_b.reshape(slot_count, tile_size),
        got_b.reshape(slot_count, code_width),
    )


def per_device(a_tiles, a_owner, a_offset, b_tiles, b_owner, b_offset, patch_valid):
    grid_rows, grid_cols = patch_valid.shape
    tile_h = grid_rows * STRIDE // TY
    tile_w = grid_cols * STRIDE // TX
    tile_count = a_tiles.shape[0]
    row_count = lax.axis_size("row")
    col_count = lax.axis_size("col")
    devices = row_count * col_count
    capacity = 4 * tile_count // (3 * devices)
    slot_count = devices * capacity
    send_a, code_a = outgoing(a_tiles, a_owner, a_offset, slot_count, capacity, tile_h, tile_w)
    send_b, code_b = outgoing(b_tiles, b_owner, b_offset, slot_count, capacity, tile_h, tile_w)
    recv_a, got_a, recv_b, got_b = route(
        send_a, code_a, send_b, code_b, row_count, col_count, capacity
    )
    canvas_a = incoming(recv_a, got_a, tile_count, tile_h, tile_w)
    canvas_b = incoming(recv_b, got_b, tile_count, tile_h, tile_w)
    images = jnp.stack([canvas_a, canvas_b])
    padded = extended_2(images, (("row", 1), ("col", 2)), MARGIN)
    padded = jnp.pad(
        padded, ((0, 0), (0, ROWS - padded.shape[1]), (0, COLS - padded.shape[2]))
    )
    confidence, flow_y, flow_x = correlate(padded, grid_rows, grid_cols)
    flow_field = jnp.stack([flow_y, flow_x])
    valid_float = patch_valid.astype(jnp.float32)
    strength = valid_float * confidence
    data_pull = strength[None] * flow_field
    initial = valid_float[None] * flow_field
    fields = jnp.concatenate(
        [strength[None], data_pull, initial, jnp.ones_like(strength)[None]], axis=0
    )
    extended = extended_2(fields, (("row", 1), ("col", 2)), SWEEPS)
    mesh_field = extended[3:5]
    for sweep_index in range(SWEEPS):
        edge = sweep_index + 1
        inner_rows = extended.shape[1] - 2 * edge
        inner_cols = extended.shape[2] - 2 * edge
        margin_fields = extended[:, edge : edge + inner_rows, edge : edge + inner_cols]
        beside_all = (
            mesh_field[:, :-2, 1:-1]
            + mesh_field[:, 2:, 1:-1]
            + mesh_field[:, 1:-1, :-2]
            + mesh_field[:, 1:-1, 2:]
        )
        mesh_field = margin_fields[5][None] * (
            (margin_fields[1:3] + stiffness * beside_all)
            / (margin_fields[0][None] + 4.0 * stiffness)
        )
    return (flow_field, mesh_field)


def solution(mesh):
    in_specs = (
        P(("row", "col"), None),
        P(("row", "col")),
        P(("row", "col"), None),
        P(("row", "col"), None),
        P(("row", "col")),
        P(("row", "col"), None),
        P("row", "col"),
    )
    out_specs = (P(None, "row", "col"), P(None, "row", "col"))
    return jax.shard_map(
        per_device, mesh=mesh, in_specs=in_specs, out_specs=out_specs, check_vma=False
    )
```

```python
import math

import jax
import jax.numpy as jnp
import ml_dtypes
import numpy as np
from jax import lax
from jax.experimental import pallas as pl
from jax.experimental.pallas import tpu as pltpu
from jax.sharding import PartitionSpec as P

PATCH = 160
STRIDE = 40
TY = 12
TX = 8
SWEEPS = 3
MARGIN = 60


stiffness = 1.0
tiny = 1e-06


HALF = PATCH // 2 + 1
KPAD = 88
EDGE_R = 64
EDGE_C = 128
ROWS = 608
COLS = 896
ROW0 = EDGE_R - MARGIN
COL0 = EDGE_C - MARGIN
WIN = 208
MESH = pl.DeviceIdType.MESH


def tables():
    index = np.arange(PATCH, dtype=np.int64)
    phase = (index[:, None] * index[None, :] % PATCH).astype(np.float32) * np.float32(
        2.0 * math.pi / PATCH
    )
    cos = np.cos(phase).astype(ml_dtypes.bfloat16).astype(np.float32)
    sin = np.sin(phase).astype(ml_dtypes.bfloat16).astype(np.float32)
    sin[(index[:, None] * index[None, :]) % 80 == 0] = 0.0
    first = np.zeros((2, 416, 256), np.float32)
    for parity in range(2):
        top = 132 + 8 * parity
        first[parity, top : top + PATCH, :HALF] = cos[:, :HALF]
        first[parity, top : top + PATCH, 128 : 128 + HALF] = sin[:, :HALF]
    second = np.zeros((4 * KPAD, WIN), np.float32)
    for parity in range(2):
        left = ROW0 + STRIDE * parity
        top = 2 * KPAD * parity
        second[top : top + HALF, left : left + PATCH] = cos[:HALF]
        second[top + KPAD : top + KPAD + HALF, left : left + PATCH] = sin[:HALF]
    once = np.ones(HALF, np.float32)
    once[0] = once[-1] = 0.5
    third = np.zeros((PATCH, 2 * KPAD), np.float32)
    third[:, :HALF] = cos[:, :HALF] * once
    third[:, KPAD : KPAD + HALF] = sin[:, :HALF]
    fourth = np.zeros((256, 256), np.float32)
    fourth[:HALF, :PATCH] = cos[:HALF] * (2.0 * once)[:, None]
    fourth[128 : 128 + HALF, :PATCH] = -2.0 * sin[:HALF]
    band_rows = np.zeros((16, ROWS), np.float32)
    for i in range(12):
        band_rows[i, ROW0 + STRIDE * i : ROW0 + STRIDE * i + PATCH] = 1.0
    band_cols = np.zeros((COLS, 128), np.float32)
    for j in range(16):
        band_cols[COL0 + STRIDE * j : COL0 + STRIDE * j + PATCH, j] = 1.0
    as_bf16 = [jnp.asarray(t, jnp.bfloat16) for t in (first, second, third, fourth, band_rows)]
    return (*as_bf16, jnp.asarray(band_cols, jnp.float32))


def dot(left, right):
    return jnp.dot(left, right, preferred_element_type=jnp.float32)


def correlate_kernel(
    images, first, second, third, fourth, band_rows, band_cols, flow, sure, spec, scale, parts
):
    grid_rows, grid_cols = sure.shape
    half_rows = ROWS // 2

    def first_part(step, carry):
        section = step // 2
        top = pl.multiple_of(step % 2 * half_rows, 16)
        for j in range(grid_cols):
            left = (COL0 + STRIDE * j) // 128 * 128
            inside = COL0 + STRIDE * j - left
            width = 256 if inside + PATCH <= 256 else 384
            parity = inside // 8 % 2
            base = 132 + 8 * parity - inside
            strip = images[section, pl.ds(top, half_rows), left : left + width]
            spec[section, pl.ds(top, half_rows), 256 * j : 256 * (j + 1)] = dot(
                strip, first[parity, base : base + width, :]
            ).astype(jnp.bfloat16)
        return carry

    lax.fori_loop(0, 4, first_part, 0)

    norms = []
    for section in range(2):
        values = images[section].astype(jnp.float32)
        squares = values * values
        high = squares.astype(jnp.bfloat16)
        low = (squares - high.astype(jnp.float32)).astype(jnp.bfloat16)
        by_rows = dot(band_rows[...], high) + dot(band_rows[...], low)
        total = jnp.dot(
            by_rows,
            band_cols[...],
            preferred_element_type=jnp.float32,
            precision=lax.Precision.HIGHEST,
        )
        norms.append(PATCH * jnp.sqrt(total / (PATCH * PATCH) + tiny))
    inv_norms = 1.0 / (norms[0] * norms[1])
    scale[...] = (inv_norms * (1.0 / (PATCH * PATCH))) * (inv_norms * (1.0 / (PATCH * PATCH)))

    lane = lax.broadcasted_iota(jnp.int32, (8, 256), 1)
    sublane = lax.broadcasted_iota(jnp.int32, (8, 256), 0)
    unit = 16.0 / PATCH
    shift_x = jnp.where(lane < PATCH // 2, lane, lane - PATCH).astype(jnp.float32) * unit
    shift_x = jnp.where(lane < PATCH, shift_x, 0.0)
    shift_y = (sublane + PATCH // 2).astype(jnp.float32) * unit

    def patch(spec_a, spec_b):
        def combos(s):
            a, e = s[:KPAD, :128], s[:KPAD, 128:]
            d, b = s[KPAD:, :128], s[KPAD:, 128:]
            return a - b, d + e, a + b, e - d

        ra, ia, ra_m, ia_m = combos(spec_a)
        rb, ib, rb_m, ib_m = combos(spec_b)
        real, imag = ra * rb + ia * ib, ia * rb - ra * ib
        real_m, imag_m = ra_m * rb_m + ia_m * ib_m, ia_m * rb_m - ra_m * ib_m
        upper = jnp.concatenate([real + real_m, imag + imag_m], axis=1)
        lower = jnp.concatenate([imag_m - imag, real - real_m], axis=1)
        cross = jnp.concatenate([upper, lower], axis=0).astype(jnp.bfloat16)
        inverse = dot(third[...], cross).astype(jnp.bfloat16)
        corr = dot(inverse, fourth[...])
        sum_0 = jnp.zeros((8, 256), jnp.float32)
        sum_1 = jnp.zeros((8, 256), jnp.float32)
        for block in range(PATCH // 8):
            top = (block * 8 + PATCH // 2) % PATCH
            piece = corr[top : top + 8]
            sum_0 = sum_0 + piece * piece
            sum_1 = sum_1 + sum_0
        results = []
        for part in (sum_0, shift_y * sum_0 - (8.0 * unit) * sum_1, shift_x * sum_0):
            part = part[:, :128] + part[:, 128:]
            results.append(jnp.sum(part, axis=0, keepdims=True))
        return results

    def pair_row(p, carry):
        top = pl.multiple_of(p * (2 * STRIDE), 16)

        def column(j, carry):
            left = pl.multiple_of(j * 256, 256)
            both = [
                dot(second[...], spec[section, pl.ds(top, WIN), pl.ds(left, 256)])
                for section in range(2)
            ]
            for parity in range(2):
                rows = slice(2 * KPAD * parity, 2 * KPAD * (parity + 1))
                for c, row in enumerate(patch(both[0][rows], both[1][rows])):
                    parts[c, parity, pl.ds(j, 1), :] = row
            return carry

        lax.fori_loop(0, grid_cols, column, 0, unroll=UNROLL)
        ones = jnp.ones((8, 128), jnp.float32)
        for parity in range(2):
            i = 2 * p + parity
            sums = [
                lax.dot_general(
                    ones,
                    parts[c, parity],
                    (((1,), (1,)), ((), ())),
                    preferred_element_type=jnp.float32,
                    precision=lax.Precision.HIGHEST,
                )[:1]
                * scale[pl.ds(i, 1), :grid_cols]
                for c in range(3)
            ]
            below = 1.0 + sums[0]
            sure[pl.ds(i, 1), :] = sums[0] / below
            flow[0, pl.ds(i, 1), :] = sums[1] / below
            flow[1, pl.ds(i, 1), :] = sums[2] / below
        return carry

    lax.fori_loop(0, grid_rows // 2, pair_row, 0)


UNROLL = 2


def correlate(images, grid_rows, grid_cols):
    vmem = pl.BlockSpec(memory_space=pltpu.VMEM)
    return pl.pallas_call(
        correlate_kernel,
        out_shape=(
            jax.ShapeDtypeStruct((2, grid_rows, grid_cols), jnp.float32),
            jax.ShapeDtypeStruct((grid_rows, grid_cols), jnp.float32),
        ),
        in_specs=[vmem] * 7,
        out_specs=(vmem, vmem),
        scratch_shapes=[
            pltpu.VMEM((2, ROWS, 256 * grid_cols), jnp.bfloat16),
            pltpu.VMEM((16, 128), jnp.float32),
            pltpu.VMEM((3, 2, grid_cols, 128), jnp.float32),
        ],
        compiler_params=pltpu.CompilerParams(vmem_limit_bytes=48 * 1024 * 1024),
    )(images, *tables())


DIRECTIONS = [(dr, dc) for dr in (-1, 0, 1) for dc in (-1, 0, 1) if (dr, dc) != (0, 0)]


def exists(row, col):
    return (
        (row >= 0)
        & (row < lax.axis_size("row"))
        & (col >= 0)
        & (col < lax.axis_size("col"))
    )


def greet_neighbours(row, col):
    barrier = pltpu.get_barrier_semaphore()
    for dr, dc in DIRECTIONS:

        @pl.when(exists(row + dr, col + dc))
        def _(dr=dr, dc=dc):
            pl.semaphore_signal(
                barrier, inc=1, device_id=(row + dr, col + dc), device_id_type=MESH
            )

    def along(index, axis):
        return 1 + jnp.where(index > 0, 1, 0) + jnp.where(index < lax.axis_size(axis) - 1, 1, 0)

    pl.semaphore_wait(barrier, along(row, "row") * along(col, "col") - 1)


def exchange(row, col, copies):
    for (dr, dc), copy in zip(DIRECTIONS, copies):

        @pl.when(exists(row + dr, col + dc))
        def _(copy=copy):
            copy.start()

    for (dr, dc), copy in zip(DIRECTIONS, copies):

        @pl.when(exists(row + dr, col + dc))
        def _(copy=copy):
            copy.wait_send()

        @pl.when(exists(row - dr, col - dc))
        def _(copy=copy):
            copy.wait_recv()


def halo_kernel(canvas, image, send_sem, recv_sem):
    row, col = lax.axis_index("row"), lax.axis_index("col")
    height, width = canvas.shape[1:]
    image[:, :EDGE_R, :] = jnp.zeros((2, EDGE_R, COLS), jnp.bfloat16)
    image[:, EDGE_R + height :, :] = jnp.zeros((2, EDGE_R, COLS), jnp.bfloat16)
    side = jnp.zeros((2, height, EDGE_C), jnp.bfloat16)
    image[:, EDGE_R : EDGE_R + height, :EDGE_C] = side
    image[:, EDGE_R : EDGE_R + height, EDGE_C + width :] = side
    greet_neighbours(row, col)
    rows = {
        -1: (slice(0, EDGE_R), slice(EDGE_R + height, ROWS)),
        0: (slice(0, height), slice(EDGE_R, EDGE_R + height)),
        1: (slice(height - EDGE_R, height), slice(0, EDGE_R)),
    }
    cols = {
        -1: (slice(0, EDGE_C), slice(EDGE_C + width, COLS)),
        0: (slice(0, width), slice(EDGE_C, EDGE_C + width)),
        1: (slice(width - EDGE_C, width), slice(0, EDGE_C)),
    }
    copies = [
        pltpu.make_async_remote_copy(
            src_ref=canvas.at[:, rows[dr][0], cols[dc][0]],
            dst_ref=image.at[:, rows[dr][1], cols[dc][1]],
            send_sem=send_sem.at[d],
            recv_sem=recv_sem.at[d],
            device_id=(row + dr, col + dc),
            device_id_type=MESH,
        )
        for d, (dr, dc) in enumerate(DIRECTIONS)
    ]
    image[:, EDGE_R : EDGE_R + height, EDGE_C : EDGE_C + width] = canvas[...]
    exchange(row, col, copies)


def with_halo(canvas):
    vmem = pl.BlockSpec(memory_space=pltpu.VMEM)
    return pl.pallas_call(
        halo_kernel,
        out_shape=jax.ShapeDtypeStruct((2, ROWS, COLS), jnp.bfloat16),
        in_specs=[vmem],
        out_specs=vmem,
        scratch_shapes=[pltpu.SemaphoreType.DMA((8,)), pltpu.SemaphoreType.DMA((8,))],
        compiler_params=pltpu.CompilerParams(
            collective_id=0, has_side_effects=True, vmem_limit_bytes=32 * 1024 * 1024
        ),
    )(canvas)


def mesh_kernel(flow, sure, valid, out, mine, near, send_sem, recv_sem):
    row, col = lax.axis_index("row"), lax.axis_index("col")
    grid_rows, grid_cols = valid.shape
    near[...] = jnp.zeros(near.shape, jnp.float32)
    mine[...] = jnp.zeros(mine.shape, jnp.float32)
    usable = valid[...].astype(jnp.float32)
    mine[0, :grid_rows, :grid_cols] = usable * sure[...]
    mine[1, :grid_rows, :grid_cols] = usable * flow[0]
    mine[2, :grid_rows, :grid_cols] = usable * flow[1]
    greet_neighbours(row, col)
    copies = [
        pltpu.make_async_remote_copy(
            src_ref=mine,
            dst_ref=near.at[d],
            send_sem=send_sem.at[d],
            recv_sem=recv_sem.at[d],
            device_id=(row + dr, col + dc),
            device_id_type=MESH,
        )
        for d, (dr, dc) in enumerate(DIRECTIONS)
    ]
    exchange(row, col, copies)
    shape = mine.shape[1:]
    i = lax.broadcasted_iota(jnp.int32, shape, 0)
    j = lax.broadcasted_iota(jnp.int32, shape, 1)

    def within(index, d, count):
        low = {-1: 0, 0: SWEEPS, 1: SWEEPS + count}[d]
        high = {-1: SWEEPS, 0: SWEEPS + count, 1: 2 * SWEEPS + count}[d]
        return (index >= low) & (index < high)

    def moved(block, down, right):
        if down % shape[0]:
            block = pltpu.roll(block, down % shape[0], 0)
        if right % shape[1]:
            block = pltpu.roll(block, right % shape[1], 1)
        return block

    fields = []
    for f in range(3):
        total = jnp.zeros(shape, jnp.float32)
        for dr in (-1, 0, 1):
            for dc in (-1, 0, 1):
                if (dr, dc) == (0, 0):
                    block = mine[f]
                else:
                    block = near[DIRECTIONS.index((-dr, -dc)), f]
                block = moved(block, SWEEPS + grid_rows * dr, SWEEPS + grid_cols * dc)
                here = within(i, dr, grid_rows) & within(j, dc, grid_cols)
                total = jnp.where(here, block, total)
        fields.append(total)
    strength, start_y, start_x = fields
    grid_i = row * grid_rows + i - SWEEPS
    grid_j = col * grid_cols + j - SWEEPS
    inside = (
        (grid_i >= 0)
        & (grid_i < lax.axis_size("row") * grid_rows)
        & (grid_j >= 0)
        & (grid_j < lax.axis_size("col") * grid_cols)
        & (i < grid_rows + 2 * SWEEPS)
        & (j < grid_cols + 2 * SWEEPS)
    )
    for f, start in enumerate((start_y, start_x)):
        pull = strength * start
        field = start
        for _ in range(SWEEPS):
            around = moved(field, 1, 0) + moved(field, -1, 0)
            around = around + moved(field, 0, 1) + moved(field, 0, -1)
            field = (pull + stiffness * around) / (strength + 4.0 * stiffness)
            field = jnp.where(inside, field, 0.0)
        out[f] = moved(field, -SWEEPS, -SWEEPS)[:grid_rows, :grid_cols]


def relaxed(flow, sure, valid):
    vmem = pl.BlockSpec(memory_space=pltpu.VMEM)
    return pl.pallas_call(
        mesh_kernel,
        out_shape=jax.ShapeDtypeStruct(flow.shape, jnp.float32),
        in_specs=[vmem] * 3,
        out_specs=vmem,
        scratch_shapes=[
            pltpu.VMEM((3, 24, 128), jnp.float32),
            pltpu.VMEM((8, 3, 24, 128), jnp.float32),
            pltpu.SemaphoreType.DMA((8,)),
            pltpu.SemaphoreType.DMA((8,)),
        ],
        compiler_params=pltpu.CompilerParams(collective_id=1, has_side_effects=True),
    )(flow, sure, valid)


def slots(tile_owner):
    index = jnp.arange(tile_owner.shape[0], dtype=jnp.int32)
    earlier = (tile_owner[:, None] == tile_owner[None, :]) & (index[:, None] > index[None, :])
    return tile_owner, jnp.sum(earlier.astype(jnp.int32), axis=1)


def routed(tiles, owners, offsets, devices, capacity, tile_h, tile_w):
    tile_count, tile_size = tiles[0].shape
    targets, rows = [], []
    for section in range(2):
        owner, rank = slots(owners[section])
        targets.append(owner * (2 * capacity) + section * capacity + rank)
        offset = offsets[section]
        place = offset[:, 0] // tile_h * TX + offset[:, 1] // tile_w + 1
        code = jnp.pad(place.astype(jnp.bfloat16)[:, None], ((0, 0), (0, 127)))
        rows.append(jnp.concatenate([tiles[section], code], axis=1))
    target = jnp.concatenate(targets)
    slot = jnp.arange(devices * 2 * capacity, dtype=jnp.int32)
    select = (slot[:, None] == target[None, :]).astype(jnp.bfloat16)
    sent = jnp.dot(
        select, jnp.concatenate(rows, axis=0), preferred_element_type=jnp.float32
    ).astype(jnp.bfloat16)
    got = lax.all_to_all(
        sent.reshape(devices, 2 * capacity, tile_size + 128),
        ("row", "col"),
        split_axis=0,
        concat_axis=0,
        tiled=True,
    ).reshape(devices * 2 * capacity, tile_size + 128)
    came = slot // capacity % 2 * tile_count + got[:, tile_size].astype(jnp.int32) - 1
    came = jnp.where(got[:, tile_size] > 0, came, -1)
    wanted = jnp.arange(2 * tile_count, dtype=jnp.int32)
    select = (came[None, :] == wanted[:, None]).astype(jnp.bfloat16)
    blocks = jnp.dot(
        select, got[:, :tile_size], preferred_element_type=jnp.float32
    ).astype(jnp.bfloat16)
    return (
        blocks.reshape(2, TY, TX, tile_h, tile_w)
        .transpose(0, 1, 3, 2, 4)
        .reshape(2, TY * tile_h, TX * tile_w)
    )


def per_device(a_tiles, a_owner, a_offset, b_tiles, b_owner, b_offset, patch_valid):
    grid_rows, grid_cols = patch_valid.shape
    tile_h = grid_rows * STRIDE // TY
    tile_w = grid_cols * STRIDE // TX
    devices = lax.axis_size("row") * lax.axis_size("col")
    capacity = 4 * a_tiles.shape[0] // (3 * devices)
    canvas = routed(
        (a_tiles, b_tiles),
        (a_owner, b_owner),
        (a_offset, b_offset),
        devices,
        capacity,
        tile_h,
        tile_w,
    )
    flow_field, confidence = correlate(with_halo(canvas), grid_rows, grid_cols)
    return flow_field, relaxed(flow_field, confidence, patch_valid)


def solution(mesh):
    in_specs = (
        P(("row", "col"), None),
        P(("row", "col")),
        P(("row", "col"), None),
        P(("row", "col"), None),
        P(("row", "col")),
        P(("row", "col"), None),
        P("row", "col"),
    )
    out_specs = (P(None, "row", "col"), P(None, "row", "col"))
    return jax.shard_map(
        per_device, mesh=mesh, in_specs=in_specs, out_specs=out_specs, check_vma=False
    )
```

```python
import math

import jax
import jax.numpy as jnp
import ml_dtypes
import numpy as np
from jax import lax
from jax.experimental import pallas as pl
from jax.experimental.pallas import tpu as pltpu
from jax.sharding import PartitionSpec as P

PATCH = 160
STRIDE = 40
TY = 12
TX = 8
SWEEPS = 3
MARGIN = 60


stiffness = 1.0
tiny = 1e-06


HALF = PATCH // 2 + 1
KPAD = 88
EDGE_R = 64
EDGE_C = 128
ROWS = 608
COLS = 896
ROW0 = EDGE_R - MARGIN
COL0 = EDGE_C - MARGIN
WIN = 208
MESH = pl.DeviceIdType.MESH


def tables():
    index = np.arange(PATCH, dtype=np.int64)
    phase = (index[:, None] * index[None, :] % PATCH).astype(np.float32) * np.float32(
        2.0 * math.pi / PATCH
    )
    cos = np.cos(phase).astype(ml_dtypes.bfloat16).astype(np.float32)
    sin = np.sin(phase).astype(ml_dtypes.bfloat16).astype(np.float32)
    sin[(index[:, None] * index[None, :]) % 80 == 0] = 0.0
    first = np.zeros((2, 416, 256), np.float32)
    for parity in range(2):
        top = 132 + 8 * parity
        first[parity, top : top + PATCH, :HALF] = cos[:, :HALF]
        first[parity, top : top + PATCH, 128 : 128 + HALF] = sin[:, :HALF]
    second = np.zeros((4 * KPAD, WIN), np.float32)
    for parity in range(2):
        left = ROW0 + STRIDE * parity
        top = 2 * KPAD * parity
        second[top : top + HALF, left : left + PATCH] = cos[:HALF]
        second[top + KPAD : top + KPAD + HALF, left : left + PATCH] = sin[:HALF]
    once = np.ones(HALF, np.float32)
    once[0] = once[-1] = 0.5
    third = np.zeros((PATCH, 2 * KPAD), np.float32)
    third[:, :HALF] = cos[:, :HALF] * once
    third[:, KPAD : KPAD + HALF] = sin[:, :HALF]
    fourth = np.zeros((256, 256), np.float32)
    fourth[:HALF, :PATCH] = cos[:HALF] * (2.0 * once)[:, None]
    fourth[128 : 128 + HALF, :PATCH] = -2.0 * sin[:HALF]
    band_rows = np.zeros((16, ROWS), np.float32)
    for i in range(12):
        band_rows[i, ROW0 + STRIDE * i : ROW0 + STRIDE * i + PATCH] = 1.0
    band_cols = np.zeros((COLS, 128), np.float32)
    for j in range(16):
        band_cols[COL0 + STRIDE * j : COL0 + STRIDE * j + PATCH, j] = 1.0
    as_bf16 = [jnp.asarray(t, jnp.bfloat16) for t in (first, second, third, fourth, band_rows)]
    return (*as_bf16, jnp.asarray(band_cols, jnp.float32))


def dot(left, right):
    return jnp.dot(left, right, preferred_element_type=jnp.float32)


def correlate_kernel(
    images, first, second, third, fourth, band_rows, band_cols, flow, sure, spec, scale, parts,
    spectra_0, spectra_1, inverse_0, inverse_1,
):
    grid_rows, grid_cols = sure.shape
    half_rows = ROWS // 2

    def first_part(step, carry):
        section = step // 2
        top = pl.multiple_of(step % 2 * half_rows, 16)
        for j in range(grid_cols):
            left = (COL0 + STRIDE * j) // 128 * 128
            inside = COL0 + STRIDE * j - left
            width = 256 if inside + PATCH <= 256 else 384
            parity = inside // 8 % 2
            base = 132 + 8 * parity - inside
            strip = images[section, pl.ds(top, half_rows), left : left + width]
            spec[section, pl.ds(top, half_rows), 256 * j : 256 * (j + 1)] = dot(
                strip, first[parity, base : base + width, :]
            ).astype(jnp.bfloat16)
        return carry

    lax.fori_loop(0, 4, first_part, 0)

    norms = []
    for section in range(2):
        values = images[section].astype(jnp.float32)
        squares = values * values
        high = squares.astype(jnp.bfloat16)
        low = (squares - high.astype(jnp.float32)).astype(jnp.bfloat16)
        by_rows = dot(band_rows[...], high) + dot(band_rows[...], low)
        total = jnp.dot(
            by_rows,
            band_cols[...],
            preferred_element_type=jnp.float32,
            precision=lax.Precision.HIGHEST,
        )
        norms.append(PATCH * jnp.sqrt(total / (PATCH * PATCH) + tiny))
    inv_norms = 1.0 / (norms[0] * norms[1])
    scale[...] = (inv_norms * (1.0 / (PATCH * PATCH))) * (inv_norms * (1.0 / (PATCH * PATCH)))

    lane = lax.broadcasted_iota(jnp.int32, (8, 256), 1)
    sublane = lax.broadcasted_iota(jnp.int32, (8, 256), 0)
    unit = 16.0 / PATCH
    shift_x = jnp.where(lane < PATCH // 2, lane, lane - PATCH).astype(jnp.float32) * unit
    shift_x = jnp.where(lane < PATCH, shift_x, 0.0)
    shift_y = (sublane + PATCH // 2).astype(jnp.float32) * unit

    pairs = grid_rows // 2 * grid_cols

    def forward(t, spectra):
        t = jnp.minimum(t, pairs - 1)
        top = pl.multiple_of(t // grid_cols * (2 * STRIDE), 16)
        left = pl.multiple_of(t % grid_cols * 256, 256)
        for section in range(2):
            spectra[section] = dot(second[...], spec[section, pl.ds(top, WIN), pl.ds(left, 256)])

    def combos(spectra, section, parity):
        top = 2 * KPAD * parity
        a = spectra[section, top : top + KPAD, :128]
        e = spectra[section, top : top + KPAD, 128:]
        d = spectra[section, top + KPAD : top + 2 * KPAD, :128]
        b = spectra[section, top + KPAD : top + 2 * KPAD, 128:]
        return a - b, d + e, a + b, e - d

    def crossed(spectra, inverse):
        for parity in range(2):
            ra, ia, ra_m, ia_m = combos(spectra, 0, parity)
            rb, ib, rb_m, ib_m = combos(spectra, 1, parity)
            real, imag = ra * rb + ia * ib, ia * rb - ra * ib
            real_m, imag_m = ra_m * rb_m + ia_m * ib_m, ia_m * rb_m - ra_m * ib_m
            upper = jnp.concatenate([real + real_m, imag + imag_m], axis=1)
            lower = jnp.concatenate([imag_m - imag, real - real_m], axis=1)
            cross = jnp.concatenate([upper, lower], axis=0).astype(jnp.bfloat16)
            inverse[PATCH * parity : PATCH * (parity + 1)] = dot(third[...], cross).astype(
                jnp.bfloat16
            )

    def summed(t, inverse):
        corr = dot(inverse[...], fourth[...])
        for parity in range(2):
            sum_0 = jnp.zeros((8, 256), jnp.float32)
            sum_1 = jnp.zeros((8, 256), jnp.float32)
            for block in range(PATCH // 8):
                top = PATCH * parity + (block * 8 + PATCH // 2) % PATCH
                piece = corr[top : top + 8]
                sum_0 = sum_0 + piece * piece
                sum_1 = sum_1 + sum_0
            moments = (sum_0, shift_y * sum_0 - (8.0 * unit) * sum_1, shift_x * sum_0)
            for c, part in enumerate(moments):
                part = part[:, :128] + part[:, 128:]
                parts[c, parity, pl.ds(t + 1, 1), :] = jnp.sum(part, axis=0, keepdims=True)

    inverse_1[...] = jnp.zeros(inverse_1.shape, jnp.bfloat16)
    forward(0, spectra_0)

    def step(u, carry):
        t = 2 * u
        summed(t - 1, inverse_1)
        crossed(spectra_0, inverse_0)
        forward(t + 1, spectra_1)
        summed(t, inverse_0)
        crossed(spectra_1, inverse_1)
        forward(t + 2, spectra_0)
        return carry

    lax.fori_loop(0, pairs // 2, step, 0)
    summed(pairs - 1, inverse_1)

    ones = jnp.ones((8, 128), jnp.float32)
    for i in range(grid_rows):
        first_pair = i // 2 * grid_cols + 1
        sums = [
            lax.dot_general(
                ones,
                parts[c, i % 2, first_pair : first_pair + grid_cols, :],
                (((1,), (1,)), ((), ())),
                preferred_element_type=jnp.float32,
                precision=lax.Precision.HIGHEST,
            )[:1]
            * scale[i : i + 1, :grid_cols]
            for c in range(3)
        ]
        below = 1.0 + sums[0]
        sure[i : i + 1, :] = sums[0] / below
        flow[0, i : i + 1, :] = sums[1] / below
        flow[1, i : i + 1, :] = sums[2] / below


def correlate(images, grid_rows, grid_cols):
    vmem = pl.BlockSpec(memory_space=pltpu.VMEM)
    return pl.pallas_call(
        correlate_kernel,
        out_shape=(
            jax.ShapeDtypeStruct((2, grid_rows, grid_cols), jnp.float32),
            jax.ShapeDtypeStruct((grid_rows, grid_cols), jnp.float32),
        ),
        in_specs=[vmem] * 7,
        out_specs=(vmem, vmem),
        scratch_shapes=[
            pltpu.VMEM((2, ROWS, 256 * grid_cols), jnp.bfloat16),
            pltpu.VMEM((16, 128), jnp.float32),
            pltpu.VMEM((3, 2, grid_rows // 2 * grid_cols + 8, 128), jnp.float32),
            pltpu.VMEM((2, 4 * KPAD, 256), jnp.float32),
            pltpu.VMEM((2, 4 * KPAD, 256), jnp.float32),
            pltpu.VMEM((2 * PATCH, 256), jnp.bfloat16),
            pltpu.VMEM((2 * PATCH, 256), jnp.bfloat16),
        ],
        compiler_params=pltpu.CompilerParams(vmem_limit_bytes=48 * 1024 * 1024),
    )(images, *tables())


DIRECTIONS = [(dr, dc) for dr in (-1, 0, 1) for dc in (-1, 0, 1) if (dr, dc) != (0, 0)]


def exists(row, col):
    return (
        (row >= 0)
        & (row < lax.axis_size("row"))
        & (col >= 0)
        & (col < lax.axis_size("col"))
    )


def greet_neighbours(row, col):
    barrier = pltpu.get_barrier_semaphore()
    for dr, dc in DIRECTIONS:

        @pl.when(exists(row + dr, col + dc))
        def _(dr=dr, dc=dc):
            pl.semaphore_signal(
                barrier, inc=1, device_id=(row + dr, col + dc), device_id_type=MESH
            )

    def along(index, axis):
        return 1 + jnp.where(index > 0, 1, 0) + jnp.where(index < lax.axis_size(axis) - 1, 1, 0)

    pl.semaphore_wait(barrier, along(row, "row") * along(col, "col") - 1)


def exchange(row, col, copies):
    for (dr, dc), copy in zip(DIRECTIONS, copies):

        @pl.when(exists(row + dr, col + dc))
        def _(copy=copy):
            copy.start()

    for (dr, dc), copy in zip(DIRECTIONS, copies):

        @pl.when(exists(row + dr, col + dc))
        def _(copy=copy):
            copy.wait_send()

        @pl.when(exists(row - dr, col - dc))
        def _(copy=copy):
            copy.wait_recv()


def halo_kernel(canvas, image, send_sem, recv_sem):
    row, col = lax.axis_index("row"), lax.axis_index("col")
    height, width = canvas.shape[1:]
    image[:, :EDGE_R, :] = jnp.zeros((2, EDGE_R, COLS), jnp.bfloat16)
    image[:, EDGE_R + height :, :] = jnp.zeros((2, EDGE_R, COLS), jnp.bfloat16)
    side = jnp.zeros((2, height, EDGE_C), jnp.bfloat16)
    image[:, EDGE_R : EDGE_R + height, :EDGE_C] = side
    image[:, EDGE_R : EDGE_R + height, EDGE_C + width :] = side
    greet_neighbours(row, col)
    rows = {
        -1: (slice(0, EDGE_R), slice(EDGE_R + height, ROWS)),
        0: (slice(0, height), slice(EDGE_R, EDGE_R + height)),
        1: (slice(height - EDGE_R, height), slice(0, EDGE_R)),
    }
    cols = {
        -1: (slice(0, EDGE_C), slice(EDGE_C + width, COLS)),
        0: (slice(0, width), slice(EDGE_C, EDGE_C + width)),
        1: (slice(width - EDGE_C, width), slice(0, EDGE_C)),
    }
    copies = [
        pltpu.make_async_remote_copy(
            src_ref=canvas.at[:, rows[dr][0], cols[dc][0]],
            dst_ref=image.at[:, rows[dr][1], cols[dc][1]],
            send_sem=send_sem.at[d],
            recv_sem=recv_sem.at[d],
            device_id=(row + dr, col + dc),
            device_id_type=MESH,
        )
        for d, (dr, dc) in enumerate(DIRECTIONS)
    ]
    image[:, EDGE_R : EDGE_R + height, EDGE_C : EDGE_C + width] = canvas[...]
    exchange(row, col, copies)


def with_halo(canvas):
    vmem = pl.BlockSpec(memory_space=pltpu.VMEM)
    return pl.pallas_call(
        halo_kernel,
        out_shape=jax.ShapeDtypeStruct((2, ROWS, COLS), jnp.bfloat16),
        in_specs=[vmem],
        out_specs=vmem,
        scratch_shapes=[pltpu.SemaphoreType.DMA((8,)), pltpu.SemaphoreType.DMA((8,))],
        compiler_params=pltpu.CompilerParams(
            collective_id=0, has_side_effects=True, vmem_limit_bytes=32 * 1024 * 1024
        ),
    )(canvas)


def mesh_kernel(flow, sure, valid, out, mine, near, send_sem, recv_sem):
    row, col = lax.axis_index("row"), lax.axis_index("col")
    grid_rows, grid_cols = valid.shape
    near[...] = jnp.zeros(near.shape, jnp.float32)
    mine[...] = jnp.zeros(mine.shape, jnp.float32)
    usable = valid[...].astype(jnp.float32)
    mine[0, :grid_rows, :grid_cols] = usable * sure[...]
    mine[1, :grid_rows, :grid_cols] = usable * flow[0]
    mine[2, :grid_rows, :grid_cols] = usable * flow[1]
    greet_neighbours(row, col)
    copies = [
        pltpu.make_async_remote_copy(
            src_ref=mine,
            dst_ref=near.at[d],
            send_sem=send_sem.at[d],
            recv_sem=recv_sem.at[d],
            device_id=(row + dr, col + dc),
            device_id_type=MESH,
        )
        for d, (dr, dc) in enumerate(DIRECTIONS)
    ]
    exchange(row, col, copies)
    shape = mine.shape[1:]
    i = lax.broadcasted_iota(jnp.int32, shape, 0)
    j = lax.broadcasted_iota(jnp.int32, shape, 1)

    def within(index, d, count):
        low = {-1: 0, 0: SWEEPS, 1: SWEEPS + count}[d]
        high = {-1: SWEEPS, 0: SWEEPS + count, 1: 2 * SWEEPS + count}[d]
        return (index >= low) & (index < high)

    def moved(block, down, right):
        if down % shape[0]:
            block = pltpu.roll(block, down % shape[0], 0)
        if right % shape[1]:
            block = pltpu.roll(block, right % shape[1], 1)
        return block

    fields = []
    for f in range(3):
        total = jnp.zeros(shape, jnp.float32)
        for dr in (-1, 0, 1):
            for dc in (-1, 0, 1):
                if (dr, dc) == (0, 0):
                    block = mine[f]
                else:
                    block = near[DIRECTIONS.index((-dr, -dc)), f]
                block = moved(block, SWEEPS + grid_rows * dr, SWEEPS + grid_cols * dc)
                here = within(i, dr, grid_rows) & within(j, dc, grid_cols)
                total = jnp.where(here, block, total)
        fields.append(total)
    strength, start_y, start_x = fields
    grid_i = row * grid_rows + i - SWEEPS
    grid_j = col * grid_cols + j - SWEEPS
    inside = (
        (grid_i >= 0)
        & (grid_i < lax.axis_size("row") * grid_rows)
        & (grid_j >= 0)
        & (grid_j < lax.axis_size("col") * grid_cols)
        & (i < grid_rows + 2 * SWEEPS)
        & (j < grid_cols + 2 * SWEEPS)
    )
    for f, start in enumerate((start_y, start_x)):
        pull = strength * start
        field = start
        for _ in range(SWEEPS):
            around = moved(field, 1, 0) + moved(field, -1, 0)
            around = around + moved(field, 0, 1) + moved(field, 0, -1)
            field = (pull + stiffness * around) / (strength + 4.0 * stiffness)
            field = jnp.where(inside, field, 0.0)
        out[f] = moved(field, -SWEEPS, -SWEEPS)[:grid_rows, :grid_cols]


def relaxed(flow, sure, valid):
    vmem = pl.BlockSpec(memory_space=pltpu.VMEM)
    return pl.pallas_call(
        mesh_kernel,
        out_shape=jax.ShapeDtypeStruct(flow.shape, jnp.float32),
        in_specs=[vmem] * 3,
        out_specs=vmem,
        scratch_shapes=[
            pltpu.VMEM((3, 24, 128), jnp.float32),
            pltpu.VMEM((8, 3, 24, 128), jnp.float32),
            pltpu.SemaphoreType.DMA((8,)),
            pltpu.SemaphoreType.DMA((8,)),
        ],
        compiler_params=pltpu.CompilerParams(collective_id=1, has_side_effects=True),
    )(flow, sure, valid)


def slots(tile_owner):
    index = jnp.arange(tile_owner.shape[0], dtype=jnp.int32)
    earlier = (tile_owner[:, None] == tile_owner[None, :]) & (index[:, None] > index[None, :])
    return tile_owner, jnp.sum(earlier.astype(jnp.int32), axis=1)


def routed(tiles, owners, offsets, devices, capacity, tile_h, tile_w):
    tile_count, tile_size = tiles[0].shape
    targets, rows = [], []
    for section in range(2):
        owner, rank = slots(owners[section])
        targets.append(owner * (2 * capacity) + section * capacity + rank)
        offset = offsets[section]
        place = offset[:, 0] // tile_h * TX + offset[:, 1] // tile_w + 1
        code = jnp.pad(place.astype(jnp.bfloat16)[:, None], ((0, 0), (0, 127)))
        rows.append(jnp.concatenate([tiles[section], code], axis=1))
    target = jnp.concatenate(targets)
    slot = jnp.arange(devices * 2 * capacity, dtype=jnp.int32)
    select = (slot[:, None] == target[None, :]).astype(jnp.bfloat16)
    sent = jnp.dot(
        select, jnp.concatenate(rows, axis=0), preferred_element_type=jnp.float32
    ).astype(jnp.bfloat16)
    got = lax.all_to_all(
        sent.reshape(devices, 2 * capacity, tile_size + 128),
        ("row", "col"),
        split_axis=0,
        concat_axis=0,
        tiled=True,
    ).reshape(devices * 2 * capacity, tile_size + 128)
    came = slot // capacity % 2 * tile_count + got[:, tile_size].astype(jnp.int32) - 1
    came = jnp.where(got[:, tile_size] > 0, came, -1)
    wanted = jnp.arange(2 * tile_count, dtype=jnp.int32)
    select = (came[None, :] == wanted[:, None]).astype(jnp.bfloat16)
    blocks = jnp.dot(
        select, got[:, :tile_size], preferred_element_type=jnp.float32
    ).astype(jnp.bfloat16)
    return (
        blocks.reshape(2, TY, TX, tile_h, tile_w)
        .transpose(0, 1, 3, 2, 4)
        .reshape(2, TY * tile_h, TX * tile_w)
    )


def per_device(a_tiles, a_owner, a_offset, b_tiles, b_owner, b_offset, patch_valid):
    grid_rows, grid_cols = patch_valid.shape
    tile_h = grid_rows * STRIDE // TY
    tile_w = grid_cols * STRIDE // TX
    devices = lax.axis_size("row") * lax.axis_size("col")
    capacity = 4 * a_tiles.shape[0] // (3 * devices)
    canvas = routed(
        (a_tiles, b_tiles),
        (a_owner, b_owner),
        (a_offset, b_offset),
        devices,
        capacity,
        tile_h,
        tile_w,
    )
    flow_field, confidence = correlate(with_halo(canvas), grid_rows, grid_cols)
    return flow_field, relaxed(flow_field, confidence, patch_valid)


def solution(mesh):
    in_specs = (
        P(("row", "col"), None),
        P(("row", "col")),
        P(("row", "col"), None),
        P(("row", "col"), None),
        P(("row", "col")),
        P(("row", "col"), None),
        P("row", "col"),
    )
    out_specs = (P(None, "row", "col"), P(None, "row", "col"))
    return jax.shard_map(
        per_device, mesh=mesh, in_specs=in_specs, out_specs=out_specs, check_vma=False
    )
```

```python
import functools
import math

import jax
import jax.numpy as jnp
import ml_dtypes
import numpy as np
from jax import lax
from jax.experimental import pallas as pl
from jax.experimental.pallas import tpu as pltpu
from jax.sharding import PartitionSpec as P

PATCH = 160
STRIDE = 40
TY = 12
TX = 8
SWEEPS = 3
MARGIN = 60


stiffness = 1.0
tiny = 1e-06


HALF = PATCH // 2 + 1
KPAD = 88
EDGE_R = 64
EDGE_C = 128
ROWS = 608
COLS = 896
ROW0 = EDGE_R - MARGIN
COL0 = EDGE_C - MARGIN
WIN = 208
MESH = pl.DeviceIdType.MESH


def tables():
    index = np.arange(PATCH, dtype=np.int64)
    phase = (index[:, None] * index[None, :] % PATCH).astype(np.float32) * np.float32(
        2.0 * math.pi / PATCH
    )
    cos = np.cos(phase).astype(ml_dtypes.bfloat16).astype(np.float32)
    sin = np.sin(phase).astype(ml_dtypes.bfloat16).astype(np.float32)
    sin[(index[:, None] * index[None, :]) % 80 == 0] = 0.0
    first = np.zeros((2, 416, 256), np.float32)
    for parity in range(2):
        top = 132 + 8 * parity
        first[parity, top : top + PATCH, :HALF] = cos[:, :HALF]
        first[parity, top : top + PATCH, 128 : 128 + HALF] = sin[:, :HALF]
    second = np.zeros((4 * KPAD, WIN), np.float32)
    for parity in range(2):
        left = ROW0 + STRIDE * parity
        top = 2 * KPAD * parity
        second[top : top + HALF, left : left + PATCH] = cos[:HALF]
        second[top + KPAD : top + KPAD + HALF, left : left + PATCH] = sin[:HALF]
    once = np.ones(HALF, np.float32)
    once[0] = once[-1] = 0.5
    third = np.zeros((PATCH, 2 * KPAD), np.float32)
    third[:, :HALF] = cos[:, :HALF] * once
    third[:, KPAD : KPAD + HALF] = sin[:, :HALF]
    fourth = np.zeros((256, 256), np.float32)
    fourth[:HALF, :PATCH] = cos[:HALF] * (2.0 * once)[:, None]
    fourth[128 : 128 + HALF, :PATCH] = -2.0 * sin[:HALF]
    band_rows = np.zeros((16, ROWS), np.float32)
    for i in range(12):
        band_rows[i, ROW0 + STRIDE * i : ROW0 + STRIDE * i + PATCH] = 1.0
    band_cols = np.zeros((COLS, 128), np.float32)
    for j in range(16):
        band_cols[COL0 + STRIDE * j : COL0 + STRIDE * j + PATCH, j] = 1.0
    as_bf16 = [jnp.asarray(t, jnp.bfloat16) for t in (first, second, third, fourth, band_rows)]
    return (*as_bf16, jnp.asarray(band_cols, jnp.float32))


def dot(left, right):
    return jnp.dot(left, right, preferred_element_type=jnp.float32)


def correlate_kernel(
    images, first, second, third, fourth, band_rows, band_cols, flow, sure, spec, scale, parts,
    spectra_0, spectra_1, inverse_0, inverse_1,
):
    grid_rows, grid_cols = sure.shape
    half_rows = ROWS // 2

    def first_part(step, carry):
        section = step // 2
        top = pl.multiple_of(step % 2 * half_rows, 16)
        for j in range(grid_cols):
            left = (COL0 + STRIDE * j) // 128 * 128
            inside = COL0 + STRIDE * j - left
            width = 256 if inside + PATCH <= 256 else 384
            parity = inside // 8 % 2
            base = 132 + 8 * parity - inside
            strip = images[section, pl.ds(top, half_rows), left : left + width]
            spec[section, pl.ds(top, half_rows), 256 * j : 256 * (j + 1)] = dot(
                strip, first[parity, base : base + width, :]
            ).astype(jnp.bfloat16)
        return carry

    lax.fori_loop(0, 4, first_part, 0)

    norms = []
    for section in range(2):
        values = images[section].astype(jnp.float32)
        squares = values * values
        high = squares.astype(jnp.bfloat16)
        low = (squares - high.astype(jnp.float32)).astype(jnp.bfloat16)
        by_rows = dot(band_rows[...], high) + dot(band_rows[...], low)
        total = jnp.dot(
            by_rows,
            band_cols[...],
            preferred_element_type=jnp.float32,
            precision=lax.Precision.HIGHEST,
        )
        norms.append(PATCH * jnp.sqrt(total / (PATCH * PATCH) + tiny))
    inv_norms = 1.0 / (norms[0] * norms[1])
    scale[...] = (inv_norms * (1.0 / (PATCH * PATCH))) * (inv_norms * (1.0 / (PATCH * PATCH)))

    lane = lax.broadcasted_iota(jnp.int32, (8, 256), 1)
    sublane = lax.broadcasted_iota(jnp.int32, (8, 256), 0)
    unit = 16.0 / PATCH
    shift_x = jnp.where(lane < PATCH // 2, lane, lane - PATCH).astype(jnp.float32) * unit
    shift_x = jnp.where(lane < PATCH, shift_x, 0.0)
    shift_y = (sublane + PATCH // 2).astype(jnp.float32) * unit

    pairs = grid_rows // 2 * grid_cols

    def forward(t, spectra):
        t = jnp.minimum(t, pairs - 1)
        top = pl.multiple_of(t // grid_cols * (2 * STRIDE), 16)
        left = pl.multiple_of(t % grid_cols * 256, 256)
        for section in range(2):
            spectra[section] = dot(second[...], spec[section, pl.ds(top, WIN), pl.ds(left, 256)])

    def combos(spectra, section, parity):
        top = 2 * KPAD * parity
        a = spectra[section, top : top + KPAD, :128]
        e = spectra[section, top : top + KPAD, 128:]
        d = spectra[section, top + KPAD : top + 2 * KPAD, :128]
        b = spectra[section, top + KPAD : top + 2 * KPAD, 128:]
        return a - b, d + e, a + b, e - d

    def crossed(spectra, inverse):
        for parity in range(2):
            ra, ia, ra_m, ia_m = combos(spectra, 0, parity)
            rb, ib, rb_m, ib_m = combos(spectra, 1, parity)
            real, imag = ra * rb + ia * ib, ia * rb - ra * ib
            real_m, imag_m = ra_m * rb_m + ia_m * ib_m, ia_m * rb_m - ra_m * ib_m
            upper = jnp.concatenate([real + real_m, imag + imag_m], axis=1)
            lower = jnp.concatenate([imag_m - imag, real - real_m], axis=1)
            cross = jnp.concatenate([upper, lower], axis=0).astype(jnp.bfloat16)
            inverse[PATCH * parity : PATCH * (parity + 1)] = dot(third[...], cross).astype(
                jnp.bfloat16
            )

    def summed(t, inverse):
        corr = dot(inverse[...], fourth[...])
        for parity in range(2):
            sum_0 = jnp.zeros((8, 256), jnp.float32)
            sum_1 = jnp.zeros((8, 256), jnp.float32)
            for block in range(PATCH // 8):
                top = PATCH * parity + (block * 8 + PATCH // 2) % PATCH
                piece = corr[top : top + 8]
                sum_0 = sum_0 + piece * piece
                sum_1 = sum_1 + sum_0
            moments = (sum_0, shift_y * sum_0 - (8.0 * unit) * sum_1, shift_x * sum_0)
            for c, part in enumerate(moments):
                part = part[:, :128] + part[:, 128:]
                parts[c, parity, pl.ds(t + 1, 1), :] = jnp.sum(part, axis=0, keepdims=True)

    inverse_1[...] = jnp.zeros(inverse_1.shape, jnp.bfloat16)
    forward(0, spectra_0)

    def step(u, carry):
        t = 2 * u
        summed(t - 1, inverse_1)
        crossed(spectra_0, inverse_0)
        forward(t + 1, spectra_1)
        summed(t, inverse_0)
        crossed(spectra_1, inverse_1)
        forward(t + 2, spectra_0)
        return carry

    lax.fori_loop(0, pairs // 2, step, 0)
    summed(pairs - 1, inverse_1)

    ones = jnp.ones((8, 128), jnp.float32)
    for i in range(grid_rows):
        first_pair = i // 2 * grid_cols + 1
        sums = [
            lax.dot_general(
                ones,
                parts[c, i % 2, first_pair : first_pair + grid_cols, :],
                (((1,), (1,)), ((), ())),
                preferred_element_type=jnp.float32,
                precision=lax.Precision.HIGHEST,
            )[:1]
            * scale[i : i + 1, :grid_cols]
            for c in range(3)
        ]
        below = 1.0 + sums[0]
        sure[i : i + 1, :] = sums[0] / below
        flow[0, i : i + 1, :] = sums[1] / below
        flow[1, i : i + 1, :] = sums[2] / below


def correlate(images, grid_rows, grid_cols):
    vmem = pl.BlockSpec(memory_space=pltpu.VMEM)
    return pl.pallas_call(
        correlate_kernel,
        out_shape=(
            jax.ShapeDtypeStruct((2, grid_rows, grid_cols), jnp.float32),
            jax.ShapeDtypeStruct((grid_rows, grid_cols), jnp.float32),
        ),
        in_specs=[vmem] * 7,
        out_specs=(vmem, vmem),
        scratch_shapes=[
            pltpu.VMEM((2, ROWS, 256 * grid_cols), jnp.bfloat16),
            pltpu.VMEM((16, 128), jnp.float32),
            pltpu.VMEM((3, 2, grid_rows // 2 * grid_cols + 8, 128), jnp.float32),
            pltpu.VMEM((2, 4 * KPAD, 256), jnp.float32),
            pltpu.VMEM((2, 4 * KPAD, 256), jnp.float32),
            pltpu.VMEM((2 * PATCH, 256), jnp.bfloat16),
            pltpu.VMEM((2 * PATCH, 256), jnp.bfloat16),
        ],
        compiler_params=pltpu.CompilerParams(vmem_limit_bytes=48 * 1024 * 1024),
    )(images, *tables())


DIRECTIONS = [(dr, dc) for dr in (-1, 0, 1) for dc in (-1, 0, 1) if (dr, dc) != (0, 0)]


def exists(row, col):
    return (
        (row >= 0)
        & (row < lax.axis_size("row"))
        & (col >= 0)
        & (col < lax.axis_size("col"))
    )


def greet_neighbours(row, col):
    barrier = pltpu.get_barrier_semaphore()
    for dr, dc in DIRECTIONS:

        @pl.when(exists(row + dr, col + dc))
        def _(dr=dr, dc=dc):
            pl.semaphore_signal(
                barrier, inc=1, device_id=(row + dr, col + dc), device_id_type=MESH
            )

    def along(index, axis):
        return 1 + jnp.where(index > 0, 1, 0) + jnp.where(index < lax.axis_size(axis) - 1, 1, 0)

    pl.semaphore_wait(barrier, along(row, "row") * along(col, "col") - 1)


def exchange(row, col, copies):
    for (dr, dc), copy in zip(DIRECTIONS, copies):

        @pl.when(exists(row + dr, col + dc))
        def _(copy=copy):
            copy.start()

    for (dr, dc), copy in zip(DIRECTIONS, copies):

        @pl.when(exists(row + dr, col + dc))
        def _(copy=copy):
            copy.wait_send()

        @pl.when(exists(row - dr, col - dc))
        def _(copy=copy):
            copy.wait_recv()


def halo_kernel(canvas, image, send_sem, recv_sem):
    row, col = lax.axis_index("row"), lax.axis_index("col")
    height, width = canvas.shape[1:]
    image[:, :EDGE_R, :] = jnp.zeros((2, EDGE_R, COLS), jnp.bfloat16)
    image[:, EDGE_R + height :, :] = jnp.zeros((2, EDGE_R, COLS), jnp.bfloat16)
    side = jnp.zeros((2, height, EDGE_C), jnp.bfloat16)
    image[:, EDGE_R : EDGE_R + height, :EDGE_C] = side
    image[:, EDGE_R : EDGE_R + height, EDGE_C + width :] = side
    greet_neighbours(row, col)
    rows = {
        -1: (slice(0, EDGE_R), slice(EDGE_R + height, ROWS)),
        0: (slice(0, height), slice(EDGE_R, EDGE_R + height)),
        1: (slice(height - EDGE_R, height), slice(0, EDGE_R)),
    }
    cols = {
        -1: (slice(0, EDGE_C), slice(EDGE_C + width, COLS)),
        0: (slice(0, width), slice(EDGE_C, EDGE_C + width)),
        1: (slice(width - EDGE_C, width), slice(0, EDGE_C)),
    }
    copies = [
        pltpu.make_async_remote_copy(
            src_ref=canvas.at[:, rows[dr][0], cols[dc][0]],
            dst_ref=image.at[:, rows[dr][1], cols[dc][1]],
            send_sem=send_sem.at[d],
            recv_sem=recv_sem.at[d],
            device_id=(row + dr, col + dc),
            device_id_type=MESH,
        )
        for d, (dr, dc) in enumerate(DIRECTIONS)
    ]
    image[:, EDGE_R : EDGE_R + height, EDGE_C : EDGE_C + width] = canvas[...]
    exchange(row, col, copies)


def with_halo(canvas):
    vmem = pl.BlockSpec(memory_space=pltpu.VMEM)
    return pl.pallas_call(
        halo_kernel,
        out_shape=jax.ShapeDtypeStruct((2, ROWS, COLS), jnp.bfloat16),
        in_specs=[vmem],
        out_specs=vmem,
        scratch_shapes=[pltpu.SemaphoreType.DMA((8,)), pltpu.SemaphoreType.DMA((8,))],
        compiler_params=pltpu.CompilerParams(
            collective_id=0, has_side_effects=True, vmem_limit_bytes=32 * 1024 * 1024
        ),
    )(canvas)


def mesh_kernel(flow, sure, valid, out, mine, near, send_sem, recv_sem):
    row, col = lax.axis_index("row"), lax.axis_index("col")
    grid_rows, grid_cols = valid.shape
    near[...] = jnp.zeros(near.shape, jnp.float32)
    mine[...] = jnp.zeros(mine.shape, jnp.float32)
    usable = valid[...].astype(jnp.float32)
    mine[0, :grid_rows, :grid_cols] = usable * sure[...]
    mine[1, :grid_rows, :grid_cols] = usable * flow[0]
    mine[2, :grid_rows, :grid_cols] = usable * flow[1]
    greet_neighbours(row, col)
    copies = [
        pltpu.make_async_remote_copy(
            src_ref=mine,
            dst_ref=near.at[d],
            send_sem=send_sem.at[d],
            recv_sem=recv_sem.at[d],
            device_id=(row + dr, col + dc),
            device_id_type=MESH,
        )
        for d, (dr, dc) in enumerate(DIRECTIONS)
    ]
    exchange(row, col, copies)
    shape = mine.shape[1:]
    i = lax.broadcasted_iota(jnp.int32, shape, 0)
    j = lax.broadcasted_iota(jnp.int32, shape, 1)

    def within(index, d, count):
        low = {-1: 0, 0: SWEEPS, 1: SWEEPS + count}[d]
        high = {-1: SWEEPS, 0: SWEEPS + count, 1: 2 * SWEEPS + count}[d]
        return (index >= low) & (index < high)

    def moved(block, down, right):
        if down % shape[0]:
            block = pltpu.roll(block, down % shape[0], 0)
        if right % shape[1]:
            block = pltpu.roll(block, right % shape[1], 1)
        return block

    fields = []
    for f in range(3):
        total = jnp.zeros(shape, jnp.float32)
        for dr in (-1, 0, 1):
            for dc in (-1, 0, 1):
                if (dr, dc) == (0, 0):
                    block = mine[f]
                else:
                    block = near[DIRECTIONS.index((-dr, -dc)), f]
                block = moved(block, SWEEPS + grid_rows * dr, SWEEPS + grid_cols * dc)
                here = within(i, dr, grid_rows) & within(j, dc, grid_cols)
                total = jnp.where(here, block, total)
        fields.append(total)
    strength, start_y, start_x = fields
    grid_i = row * grid_rows + i - SWEEPS
    grid_j = col * grid_cols + j - SWEEPS
    inside = (
        (grid_i >= 0)
        & (grid_i < lax.axis_size("row") * grid_rows)
        & (grid_j >= 0)
        & (grid_j < lax.axis_size("col") * grid_cols)
        & (i < grid_rows + 2 * SWEEPS)
        & (j < grid_cols + 2 * SWEEPS)
    )
    for f, start in enumerate((start_y, start_x)):
        pull = strength * start
        field = start
        for _ in range(SWEEPS):
            around = moved(field, 1, 0) + moved(field, -1, 0)
            around = around + moved(field, 0, 1) + moved(field, 0, -1)
            field = (pull + stiffness * around) / (strength + 4.0 * stiffness)
            field = jnp.where(inside, field, 0.0)
        out[f] = moved(field, -SWEEPS, -SWEEPS)[:grid_rows, :grid_cols]


def relaxed(flow, sure, valid):
    vmem = pl.BlockSpec(memory_space=pltpu.VMEM)
    return pl.pallas_call(
        mesh_kernel,
        out_shape=jax.ShapeDtypeStruct(flow.shape, jnp.float32),
        in_specs=[vmem] * 3,
        out_specs=vmem,
        scratch_shapes=[
            pltpu.VMEM((3, 24, 128), jnp.float32),
            pltpu.VMEM((8, 3, 24, 128), jnp.float32),
            pltpu.SemaphoreType.DMA((8,)),
            pltpu.SemaphoreType.DMA((8,)),
        ],
        compiler_params=pltpu.CompilerParams(collective_id=1, has_side_effects=True),
    )(flow, sure, valid)


MSG_ROWS = 16
CUT = 1536
MSG_COLS = 1664


def route_kernel(
    a_tiles, b_tiles, owners, offsets, out, send, recv, code_rows, send_sem, recv_sem,
    *, capacity, tile_h, tile_w,
):
    row, col = lax.axis_index("row"), lax.axis_index("col")
    col_count = lax.axis_size("col")
    devices = lax.axis_size("row") * col_count
    me = row * col_count + col
    tile_count = a_tiles.shape[0]
    chunk = 128 // MSG_ROWS
    barrier = pltpu.get_barrier_semaphore()

    def device(k):
        target = lax.rem(me + k, devices)
        return (lax.div(target, col_count), lax.rem(target, col_count))

    def greet(k, carry):
        pl.semaphore_signal(barrier, inc=1, device_id=device(k), device_id_type=MESH)
        return carry

    lax.fori_loop(1, devices, greet, 0)

    def copy(k):
        return pltpu.make_async_remote_copy(
            src_ref=send.at[k],
            dst_ref=recv.at[k],
            send_sem=send_sem.at[k],
            recv_sem=recv_sem.at[k],
            device_id=device(k),
            device_id_type=MESH,
        )

    earlier = lax.broadcasted_iota(jnp.int32, (tile_count, tile_count), 0)
    later = lax.broadcasted_iota(jnp.int32, (tile_count, tile_count), 1)
    targets, places = [], []
    for section in range(2):
        across = owners[section : section + 1, :].astype(jnp.float32)
        down = jnp.sum(jnp.where(earlier == later, across, 0.0), axis=1, keepdims=True)
        same = (down == across) & (earlier < later)
        rank = jnp.sum(jnp.where(same, 1.0, 0.0), axis=0, keepdims=True)
        ahead = across - me.astype(jnp.float32)
        ahead = jnp.where(ahead < 0.0, ahead + devices, ahead)
        targets.append(ahead * MSG_ROWS + rank + section * capacity)
        at = offsets[2 * section : 2 * section + 2, :].astype(jnp.float32)
        place_y = jnp.floor(at[0:1] * (1.0 / tile_h) + 0.5)
        place_x = jnp.floor(at[1:2] * (1.0 / tile_w) + 0.5)
        places.append(place_y * TX + place_x + 1.0)
    slot = lax.broadcasted_iota(jnp.int32, (128, tile_count), 0)

    def fill(c, carry):
        here = (slot + c * 128).astype(jnp.float32)
        code = jnp.zeros((128, 1), jnp.float32)
        left = jnp.zeros((128, CUT), jnp.float32)
        right = jnp.zeros((128, MSG_COLS - CUT), jnp.float32)
        for tiles, target, place in zip((a_tiles, b_tiles), targets, places):
            upper = jnp.where(here == target, 1.0, 0.0)
            lower = jnp.where(here == target + 8.0, 1.0, 0.0).astype(jnp.bfloat16)
            code = code + jnp.sum(upper * place, axis=1, keepdims=True)
            left = left + dot(upper.astype(jnp.bfloat16), tiles[:, :CUT])
            left = left + dot(lower, tiles[:, CUT : 2 * CUT])
            right = right + dot(lower, tiles[:, 2 * CUT :])
        block = pl.ds(c * chunk, chunk)
        send[block, :, :CUT] = left.astype(jnp.bfloat16).reshape(chunk, MSG_ROWS, CUT)
        send[block, :, CUT:] = (
            (right + code).astype(jnp.bfloat16).reshape(chunk, MSG_ROWS, MSG_COLS - CUT)
        )

        @pl.when(c == 0)
        def _():
            pl.semaphore_wait(barrier, devices - 1)
            recv[0] = send[0]

        def push(k, carry):
            copy(k).start()
            return carry

        lax.fori_loop(jnp.maximum(c * chunk, 1), (c + 1) * chunk, push, 0)
        return carry

    lax.fori_loop(0, devices // chunk, fill, 0)

    def arrive(k, carry):
        copy(k).wait()
        return carry

    lax.fori_loop(1, devices, arrive, 0)

    from_row = lax.broadcasted_iota(jnp.int32, (128, 128), 0)
    to_lane = lax.broadcasted_iota(jnp.int32, (128, 128), 1)
    to_lane = jnp.where((to_lane & 15) >= 8, to_lane - 8, to_lane)
    for c in range(devices // chunk):
        codes = recv[c * chunk : (c + 1) * chunk, :, CUT:].reshape(128, 128).astype(jnp.float32)
        code_rows[:, 128 * c : 128 * (c + 1)] = jnp.sum(
            jnp.where(from_row == to_lane, codes[:, :1], 0.0), axis=0, keepdims=True
        )
    shape = (2 * tile_count, devices * MSG_ROWS)
    wanted = lax.broadcasted_iota(jnp.int32, shape, 0).astype(jnp.float32) + 1.0
    within = lax.broadcasted_iota(jnp.int32, (1, shape[1]), 1) & 15
    code = code_rows[...]
    code = jnp.where((within & 7) >= capacity, code + tile_count, code)
    code = jnp.where(code_rows[...] > 0.0, code, 0.0)
    for half, (start, size) in enumerate(((0, CUT), (CUT, MSG_COLS))):
        in_half = (within >= 8) if half else (within < 8)
        select = jnp.where(wanted == jnp.where(in_half, code, 0.0), 1.0, 0.0).astype(jnp.bfloat16)
        rows = recv[:, :, :size].reshape(shape[1], size)
        out[:, start : start + size] = dot(select, rows).astype(jnp.bfloat16)


def routed(tiles, owners, offsets, devices, capacity, tile_h, tile_w):
    tile_count, tile_size = tiles[0].shape
    vmem = pl.BlockSpec(memory_space=pltpu.VMEM)
    buffer = pltpu.VMEM((devices, MSG_ROWS, MSG_COLS), jnp.bfloat16)
    blocks = pl.pallas_call(
        functools.partial(route_kernel, capacity=capacity, tile_h=tile_h, tile_w=tile_w),
        out_shape=jax.ShapeDtypeStruct((2 * tile_count, tile_size), jnp.bfloat16),
        in_specs=[vmem] * 4,
        out_specs=vmem,
        scratch_shapes=[
            buffer,
            buffer,
            pltpu.VMEM((1, devices * MSG_ROWS), jnp.float32),
            pltpu.SemaphoreType.DMA((devices,)),
            pltpu.SemaphoreType.DMA((devices,)),
        ],
        compiler_params=pltpu.CompilerParams(
            collective_id=2, has_side_effects=True, vmem_limit_bytes=40 * 1024 * 1024
        ),
    )(
        *tiles,
        jnp.stack(owners),
        jnp.concatenate([offset.T for offset in offsets], axis=0),
    )
    return (
        blocks.reshape(2, TY, TX, tile_h, tile_w)
        .transpose(0, 1, 3, 2, 4)
        .reshape(2, TY * tile_h, TX * tile_w)
    )


def per_device(a_tiles, a_owner, a_offset, b_tiles, b_owner, b_offset, patch_valid):
    grid_rows, grid_cols = patch_valid.shape
    tile_h = grid_rows * STRIDE // TY
    tile_w = grid_cols * STRIDE // TX
    devices = lax.axis_size("row") * lax.axis_size("col")
    capacity = 4 * a_tiles.shape[0] // (3 * devices)
    canvas = routed(
        (a_tiles, b_tiles),
        (a_owner, b_owner),
        (a_offset, b_offset),
        devices,
        capacity,
        tile_h,
        tile_w,
    )
    flow_field, confidence = correlate(with_halo(canvas), grid_rows, grid_cols)
    return flow_field, relaxed(flow_field, confidence, patch_valid)


def solution(mesh):
    in_specs = (
        P(("row", "col"), None),
        P(("row", "col")),
        P(("row", "col"), None),
        P(("row", "col"), None),
        P(("row", "col")),
        P(("row", "col"), None),
        P("row", "col"),
    )
    out_specs = (P(None, "row", "col"), P(None, "row", "col"))
    return jax.shard_map(
        per_device, mesh=mesh, in_specs=in_specs, out_specs=out_specs, check_vma=False
    )
```

```python
import functools
import math

import jax
import jax.numpy as jnp
import ml_dtypes
import numpy as np
from jax import lax
from jax.experimental import pallas as pl
from jax.experimental.pallas import tpu as pltpu
from jax.sharding import PartitionSpec as P

PATCH = 160
STRIDE = 40
TY = 12
TX = 8
SWEEPS = 3
MARGIN = 60


stiffness = 1.0
tiny = 1e-06


HALF = PATCH // 2 + 1
KPAD = 88
EDGE_R = 64
EDGE_C = 128
ROWS = 608
COLS = 896
ROW0 = EDGE_R - MARGIN
COL0 = EDGE_C - MARGIN
WIN = 208
MESH = pl.DeviceIdType.MESH


def tables():
    index = np.arange(PATCH, dtype=np.int64)
    phase = (index[:, None] * index[None, :] % PATCH).astype(np.float32) * np.float32(
        2.0 * math.pi / PATCH
    )
    cos = np.cos(phase).astype(ml_dtypes.bfloat16).astype(np.float32)
    sin = np.sin(phase).astype(ml_dtypes.bfloat16).astype(np.float32)
    sin[(index[:, None] * index[None, :]) % 80 == 0] = 0.0
    first = np.zeros((2, 416, 256), np.float32)
    for parity in range(2):
        top = 132 + 8 * parity
        first[parity, top : top + PATCH, :HALF] = cos[:, :HALF]
        first[parity, top : top + PATCH, 128 : 128 + HALF] = sin[:, :HALF]
    second = np.zeros((4 * KPAD, WIN), np.float32)
    for parity in range(2):
        left = ROW0 + STRIDE * parity
        top = 2 * KPAD * parity
        second[top : top + HALF, left : left + PATCH] = cos[:HALF]
        second[top + KPAD : top + KPAD + HALF, left : left + PATCH] = sin[:HALF]
    once = np.ones(HALF, np.float32)
    once[0] = once[-1] = 0.5
    third = np.zeros((PATCH, 2 * KPAD), np.float32)
    third[:, :HALF] = cos[:, :HALF] * once
    third[:, KPAD : KPAD + HALF] = sin[:, :HALF]
    fourth = np.zeros((256, 256), np.float32)
    fourth[:HALF, :PATCH] = cos[:HALF] * (2.0 * once)[:, None]
    fourth[128 : 128 + HALF, :PATCH] = -2.0 * sin[:HALF]
    band_rows = np.zeros((16, ROWS), np.float32)
    for i in range(12):
        band_rows[i, ROW0 + STRIDE * i : ROW0 + STRIDE * i + PATCH] = 1.0
    band_cols = np.zeros((COLS, 128), np.float32)
    for j in range(16):
        band_cols[COL0 + STRIDE * j : COL0 + STRIDE * j + PATCH, j] = 1.0
    as_bf16 = [jnp.asarray(t, jnp.bfloat16) for t in (first, second, third, fourth, band_rows)]
    return (*as_bf16, jnp.asarray(band_cols, jnp.float32))


def dot(left, right):
    return jnp.dot(left, right, preferred_element_type=jnp.float32)


def section_kernel(
    canvas, valid, first, second, third, fourth, band_rows, band_cols, flow, mesh,
    images, spec, scale, parts, spectra_0, spectra_1, inverse_0, inverse_1,
    sure, mine, near, send_sem, recv_sem,
):
    row, col = lax.axis_index("row"), lax.axis_index("col")
    grid_rows, grid_cols = valid.shape
    height, width = canvas.shape[1:]
    near[...] = jnp.zeros(near.shape, jnp.float32)
    copies = halo_copies(canvas, images, row, col, send_sem, recv_sem)
    greet_neighbours(row, col)
    start(row, col, copies)
    images[:, EDGE_R : EDGE_R + height, EDGE_C : EDGE_C + width] = canvas[...]

    def first_part(source, section, top, count, from_lane, to_row, columns):
        for j in columns:
            left = (COL0 + STRIDE * j) // 128 * 128
            inside = COL0 + STRIDE * j - left
            width = 256 if inside + PATCH <= 256 else 384
            parity = inside // 8 % 2
            base = 132 + 8 * parity - inside
            strip = source[section, top : top + count, left - from_lane : left - from_lane + width]
            spec[section, to_row : to_row + count, 256 * j : 256 * (j + 1)] = dot(
                strip, first[parity, base : base + width, :]
            ).astype(jnp.bfloat16)

    half = height // 2
    inner = [j for j in range(2, grid_cols - 2)]
    outer = [j for j in range(grid_cols) if j not in inner]

    def first_inner(section, carry):
        for top in (0, half):
            first_part(canvas, section, top, half, EDGE_C, EDGE_R + top, inner)
        return carry

    def first_outer(section, carry):
        for top in (EDGE_R, EDGE_R + half):
            first_part(images, section, top, half, 0, top, outer)
        for top in (0, EDGE_R + height):
            first_part(images, section, top, EDGE_R, 0, top, range(grid_cols))
        return carry

    lax.fori_loop(0, 2, first_inner, 0)
    finish(row, col, copies)
    lax.fori_loop(0, 2, first_outer, 0)

    norms = []
    for section in range(2):
        values = images[section].astype(jnp.float32)
        squares = values * values
        high = squares.astype(jnp.bfloat16)
        low = (squares - high.astype(jnp.float32)).astype(jnp.bfloat16)
        by_rows = dot(band_rows[...], high) + dot(band_rows[...], low)
        total = jnp.dot(
            by_rows,
            band_cols[...],
            preferred_element_type=jnp.float32,
            precision=lax.Precision.HIGHEST,
        )
        norms.append(PATCH * jnp.sqrt(total / (PATCH * PATCH) + tiny))
    inv_norms = 1.0 / (norms[0] * norms[1])
    scale[...] = (inv_norms * (1.0 / (PATCH * PATCH))) * (inv_norms * (1.0 / (PATCH * PATCH)))

    lane = lax.broadcasted_iota(jnp.int32, (8, 256), 1)
    sublane = lax.broadcasted_iota(jnp.int32, (8, 256), 0)
    unit = 16.0 / PATCH
    shift_x = jnp.where(lane < PATCH // 2, lane, lane - PATCH).astype(jnp.float32) * unit
    shift_x = jnp.where(lane < PATCH, shift_x, 0.0)
    shift_y = (sublane + PATCH // 2).astype(jnp.float32) * unit

    pairs = grid_rows // 2 * grid_cols

    def forward(t, spectra):
        t = jnp.minimum(t, pairs - 1)
        top = pl.multiple_of(t // grid_cols * (2 * STRIDE), 16)
        left = pl.multiple_of(t % grid_cols * 256, 256)
        for section in range(2):
            spectra[section] = dot(second[...], spec[section, pl.ds(top, WIN), pl.ds(left, 256)])

    def combos(spectra, section, parity):
        top = 2 * KPAD * parity
        a = spectra[section, top : top + KPAD, :128]
        e = spectra[section, top : top + KPAD, 128:]
        d = spectra[section, top + KPAD : top + 2 * KPAD, :128]
        b = spectra[section, top + KPAD : top + 2 * KPAD, 128:]
        return a - b, d + e, a + b, e - d

    def crossed(spectra, inverse):
        for parity in range(2):
            ra, ia, ra_m, ia_m = combos(spectra, 0, parity)
            rb, ib, rb_m, ib_m = combos(spectra, 1, parity)
            real, imag = ra * rb + ia * ib, ia * rb - ra * ib
            real_m, imag_m = ra_m * rb_m + ia_m * ib_m, ia_m * rb_m - ra_m * ib_m
            upper = jnp.concatenate([real + real_m, imag + imag_m], axis=1)
            lower = jnp.concatenate([imag_m - imag, real - real_m], axis=1)
            cross = jnp.concatenate([upper, lower], axis=0).astype(jnp.bfloat16)
            inverse[PATCH * parity : PATCH * (parity + 1)] = dot(third[...], cross).astype(
                jnp.bfloat16
            )

    def summed(t, inverse):
        corr = dot(inverse[...], fourth[...])
        for parity in range(2):
            sum_0 = jnp.zeros((8, 256), jnp.float32)
            sum_1 = jnp.zeros((8, 256), jnp.float32)
            for block in range(PATCH // 8):
                top = PATCH * parity + (block * 8 + PATCH // 2) % PATCH
                piece = corr[top : top + 8]
                sum_0 = sum_0 + piece * piece
                sum_1 = sum_1 + sum_0
            moments = (sum_0, shift_y * sum_0 - (8.0 * unit) * sum_1, shift_x * sum_0)
            for c, part in enumerate(moments):
                part = part[:, :128] + part[:, 128:]
                parts[c, parity, pl.ds(t + 1, 1), :] = jnp.sum(part, axis=0, keepdims=True)

    inverse_1[...] = jnp.zeros(inverse_1.shape, jnp.bfloat16)
    forward(0, spectra_0)

    def step(u, carry):
        t = 2 * u
        summed(t - 1, inverse_1)
        crossed(spectra_0, inverse_0)
        forward(t + 1, spectra_1)
        summed(t, inverse_0)
        crossed(spectra_1, inverse_1)
        forward(t + 2, spectra_0)
        return carry

    lax.fori_loop(0, pairs // 2, step, 0)
    summed(pairs - 1, inverse_1)

    ones = jnp.ones((8, 128), jnp.float32)
    for i in range(grid_rows):
        first_pair = i // 2 * grid_cols + 1
        sums = [
            lax.dot_general(
                ones,
                parts[c, i % 2, first_pair : first_pair + grid_cols, :],
                (((1,), (1,)), ((), ())),
                preferred_element_type=jnp.float32,
                precision=lax.Precision.HIGHEST,
            )[:1]
            * scale[i : i + 1, :grid_cols]
            for c in range(3)
        ]
        below = 1.0 + sums[0]
        sure[i : i + 1, :] = sums[0] / below
        flow[0, i : i + 1, :] = sums[1] / below
        flow[1, i : i + 1, :] = sums[2] / below
    relax(flow, sure, valid, mesh, mine, near, send_sem, recv_sem)


def measured(canvas, valid):
    grid_rows, grid_cols = valid.shape
    vmem = pl.BlockSpec(memory_space=pltpu.VMEM)
    field = jax.ShapeDtypeStruct((2, grid_rows, grid_cols), jnp.float32)
    return pl.pallas_call(
        section_kernel,
        out_shape=(field, field),
        in_specs=[vmem] * 8,
        out_specs=(vmem, vmem),
        scratch_shapes=[
            pltpu.VMEM((2, ROWS, COLS), jnp.bfloat16),
            pltpu.VMEM((2, ROWS, 256 * grid_cols), jnp.bfloat16),
            pltpu.VMEM((16, 128), jnp.float32),
            pltpu.VMEM((3, 2, grid_rows // 2 * grid_cols + 8, 128), jnp.float32),
            pltpu.VMEM((2, 4 * KPAD, 256), jnp.float32),
            pltpu.VMEM((2, 4 * KPAD, 256), jnp.float32),
            pltpu.VMEM((2 * PATCH, 256), jnp.bfloat16),
            pltpu.VMEM((2 * PATCH, 256), jnp.bfloat16),
            pltpu.VMEM((grid_rows, grid_cols), jnp.float32),
            pltpu.VMEM((3, 24, 128), jnp.float32),
            pltpu.VMEM((8, 3, 24, 128), jnp.float32),
            pltpu.SemaphoreType.DMA((16,)),
            pltpu.SemaphoreType.DMA((16,)),
        ],
        compiler_params=pltpu.CompilerParams(
            collective_id=0, has_side_effects=True, vmem_limit_bytes=48 * 1024 * 1024
        ),
    )(canvas, valid, *tables())


DIRECTIONS = [(dr, dc) for dr in (-1, 0, 1) for dc in (-1, 0, 1) if (dr, dc) != (0, 0)]


def exists(row, col):
    return (
        (row >= 0)
        & (row < lax.axis_size("row"))
        & (col >= 0)
        & (col < lax.axis_size("col"))
    )


def greet_neighbours(row, col):
    barrier = pltpu.get_barrier_semaphore()
    for dr, dc in DIRECTIONS:

        @pl.when(exists(row + dr, col + dc))
        def _(dr=dr, dc=dc):
            pl.semaphore_signal(
                barrier, inc=1, device_id=(row + dr, col + dc), device_id_type=MESH
            )

    def along(index, axis):
        return 1 + jnp.where(index > 0, 1, 0) + jnp.where(index < lax.axis_size(axis) - 1, 1, 0)

    pl.semaphore_wait(barrier, along(row, "row") * along(col, "col") - 1)


def start(row, col, copies):
    for (dr, dc), copy in zip(DIRECTIONS, copies):

        @pl.when(exists(row + dr, col + dc))
        def _(copy=copy):
            copy.start()


def finish(row, col, copies):
    for (dr, dc), copy in zip(DIRECTIONS, copies):

        @pl.when(exists(row + dr, col + dc))
        def _(copy=copy):
            copy.wait_send()

        @pl.when(exists(row - dr, col - dc))
        def _(copy=copy):
            copy.wait_recv()


def halo_copies(canvas, image, row, col, send_sem, recv_sem):
    height, width = canvas.shape[1:]
    image[:, :EDGE_R, :] = jnp.zeros((2, EDGE_R, COLS), jnp.bfloat16)
    image[:, EDGE_R + height :, :] = jnp.zeros((2, EDGE_R, COLS), jnp.bfloat16)
    side = jnp.zeros((2, height, EDGE_C), jnp.bfloat16)
    image[:, EDGE_R : EDGE_R + height, :EDGE_C] = side
    image[:, EDGE_R : EDGE_R + height, EDGE_C + width :] = side
    rows = {
        -1: (slice(0, EDGE_R), slice(EDGE_R + height, ROWS)),
        0: (slice(0, height), slice(EDGE_R, EDGE_R + height)),
        1: (slice(height - EDGE_R, height), slice(0, EDGE_R)),
    }
    cols = {
        -1: (slice(0, EDGE_C), slice(EDGE_C + width, COLS)),
        0: (slice(0, width), slice(EDGE_C, EDGE_C + width)),
        1: (slice(width - EDGE_C, width), slice(0, EDGE_C)),
    }
    return [
        pltpu.make_async_remote_copy(
            src_ref=canvas.at[:, rows[dr][0], cols[dc][0]],
            dst_ref=image.at[:, rows[dr][1], cols[dc][1]],
            send_sem=send_sem.at[d],
            recv_sem=recv_sem.at[d],
            device_id=(row + dr, col + dc),
            device_id_type=MESH,
        )
        for d, (dr, dc) in enumerate(DIRECTIONS)
    ]


def relax(flow, sure, valid, out, mine, near, send_sem, recv_sem):
    row, col = lax.axis_index("row"), lax.axis_index("col")
    grid_rows, grid_cols = valid.shape
    mine[...] = jnp.zeros(mine.shape, jnp.float32)
    usable = valid[...].astype(jnp.float32)
    mine[0, :grid_rows, :grid_cols] = usable * sure[...]
    mine[1, :grid_rows, :grid_cols] = usable * flow[0]
    mine[2, :grid_rows, :grid_cols] = usable * flow[1]
    copies = [
        pltpu.make_async_remote_copy(
            src_ref=mine,
            dst_ref=near.at[d],
            send_sem=send_sem.at[8 + d],
            recv_sem=recv_sem.at[8 + d],
            device_id=(row + dr, col + dc),
            device_id_type=MESH,
        )
        for d, (dr, dc) in enumerate(DIRECTIONS)
    ]
    start(row, col, copies)
    finish(row, col, copies)
    shape = mine.shape[1:]
    i = lax.broadcasted_iota(jnp.int32, shape, 0)
    j = lax.broadcasted_iota(jnp.int32, shape, 1)

    def within(index, d, count):
        low = {-1: 0, 0: SWEEPS, 1: SWEEPS + count}[d]
        high = {-1: SWEEPS, 0: SWEEPS + count, 1: 2 * SWEEPS + count}[d]
        return (index >= low) & (index < high)

    def moved(block, down, right):
        if down % shape[0]:
            block = pltpu.roll(block, down % shape[0], 0)
        if right % shape[1]:
            block = pltpu.roll(block, right % shape[1], 1)
        return block

    fields = []
    for f in range(3):
        total = jnp.zeros(shape, jnp.float32)
        for dr in (-1, 0, 1):
            for dc in (-1, 0, 1):
                if (dr, dc) == (0, 0):
                    block = mine[f]
                else:
                    block = near[DIRECTIONS.index((-dr, -dc)), f]
                block = moved(block, SWEEPS + grid_rows * dr, SWEEPS + grid_cols * dc)
                here = within(i, dr, grid_rows) & within(j, dc, grid_cols)
                total = jnp.where(here, block, total)
        fields.append(total)
    strength, start_y, start_x = fields
    grid_i = row * grid_rows + i - SWEEPS
    grid_j = col * grid_cols + j - SWEEPS
    inside = (
        (grid_i >= 0)
        & (grid_i < lax.axis_size("row") * grid_rows)
        & (grid_j >= 0)
        & (grid_j < lax.axis_size("col") * grid_cols)
        & (i < grid_rows + 2 * SWEEPS)
        & (j < grid_cols + 2 * SWEEPS)
    )
    for f, initial in enumerate((start_y, start_x)):
        pull = strength * initial
        field = initial
        for _ in range(SWEEPS):
            around = moved(field, 1, 0) + moved(field, -1, 0)
            around = around + moved(field, 0, 1) + moved(field, 0, -1)
            field = (pull + stiffness * around) / (strength + 4.0 * stiffness)
            field = jnp.where(inside, field, 0.0)
        out[f] = moved(field, -SWEEPS, -SWEEPS)[:grid_rows, :grid_cols]


MSG_ROWS = 16
CUT = 1536
MSG_COLS = 1664


def route_kernel(
    a_tiles, b_tiles, a_owner, b_owner, a_offset, b_offset, out, send, recv, code_rows, send_sem, recv_sem,
    *, capacity, tile_h, tile_w,
):
    row, col = lax.axis_index("row"), lax.axis_index("col")
    col_count = lax.axis_size("col")
    devices = lax.axis_size("row") * col_count
    me = row * col_count + col
    tile_count = a_tiles.shape[0]
    chunk = 128 // MSG_ROWS
    barrier = pltpu.get_barrier_semaphore()

    def device(k):
        target = lax.rem(me + k, devices)
        return (lax.div(target, col_count), lax.rem(target, col_count))

    def greet(k, carry):
        pl.semaphore_signal(barrier, inc=1, device_id=device(k), device_id_type=MESH)
        return carry

    lax.fori_loop(1, devices, greet, 0)

    def copy(k):
        return pltpu.make_async_remote_copy(
            src_ref=send.at[k],
            dst_ref=recv.at[k],
            send_sem=send_sem.at[k],
            recv_sem=recv_sem.at[k],
            device_id=device(k),
            device_id_type=MESH,
        )

    earlier = lax.broadcasted_iota(jnp.int32, (tile_count, tile_count), 0)
    later = lax.broadcasted_iota(jnp.int32, (tile_count, tile_count), 1)
    targets, places = [], []
    for section, (owner, offset) in enumerate(((a_owner, a_offset), (b_owner, b_offset))):
        across = owner[...].astype(jnp.float32)
        down = jnp.sum(jnp.where(earlier == later, across, 0.0), axis=1, keepdims=True)
        same = (down == across) & (earlier < later)
        rank = jnp.sum(jnp.where(same, 1.0, 0.0), axis=0, keepdims=True)
        ahead = across - me.astype(jnp.float32)
        ahead = jnp.where(ahead < 0.0, ahead + devices, ahead)
        targets.append(ahead * MSG_ROWS + rank + section * capacity)
        at = offset[...].astype(jnp.float32)
        place_y = jnp.floor(at[0:1] * (1.0 / tile_h) + 0.5)
        place_x = jnp.floor(at[1:2] * (1.0 / tile_w) + 0.5)
        places.append(place_y * TX + place_x + 1.0)
    slot = lax.broadcasted_iota(jnp.int32, (128, tile_count), 0)

    def fill(c, carry):
        here = (slot + c * 128).astype(jnp.float32)
        code = jnp.zeros((128, 1), jnp.float32)
        left = jnp.zeros((128, CUT), jnp.float32)
        right = jnp.zeros((128, MSG_COLS - CUT), jnp.float32)
        for tiles, target, place in zip((a_tiles, b_tiles), targets, places):
            upper = jnp.where(here == target, 1.0, 0.0)
            lower = jnp.where(here == target + 8.0, 1.0, 0.0).astype(jnp.bfloat16)
            code = code + jnp.sum(upper * place, axis=1, keepdims=True)
            left = left + dot(upper.astype(jnp.bfloat16), tiles[:, :CUT])
            left = left + dot(lower, tiles[:, CUT : 2 * CUT])
            right = right + dot(lower, tiles[:, 2 * CUT :])
        block = pl.ds(c * chunk, chunk)
        send[block, :, :CUT] = left.astype(jnp.bfloat16).reshape(chunk, MSG_ROWS, CUT)
        send[block, :, CUT:] = (
            (right + code).astype(jnp.bfloat16).reshape(chunk, MSG_ROWS, MSG_COLS - CUT)
        )

        @pl.when(c == 0)
        def _():
            pl.semaphore_wait(barrier, devices - 1)
            recv[0] = send[0]

        def push(k, carry):
            copy(k).start()
            return carry

        lax.fori_loop(jnp.maximum(c * chunk, 1), (c + 1) * chunk, push, 0)
        return carry

    lax.fori_loop(0, devices // chunk, fill, 0)

    def arrive(k, carry):
        copy(k).wait()
        return carry

    lax.fori_loop(1, devices, arrive, 0)

    from_row = lax.broadcasted_iota(jnp.int32, (128, 128), 0)
    to_lane = lax.broadcasted_iota(jnp.int32, (128, 128), 1)
    to_lane = jnp.where((to_lane & 15) >= 8, to_lane - 8, to_lane)
    for c in range(devices // chunk):
        codes = recv[c * chunk : (c + 1) * chunk, :, CUT:].reshape(128, 128).astype(jnp.float32)
        code_rows[:, 128 * c : 128 * (c + 1)] = jnp.sum(
            jnp.where(from_row == to_lane, codes[:, :1], 0.0), axis=0, keepdims=True
        )
    shape = (2 * tile_count, devices * MSG_ROWS)
    wanted = lax.broadcasted_iota(jnp.int32, shape, 0).astype(jnp.float32) + 1.0
    within = lax.broadcasted_iota(jnp.int32, (1, shape[1]), 1) & 15
    code = code_rows[...]
    code = jnp.where((within & 7) >= capacity, code + tile_count, code)
    code = jnp.where(code_rows[...] > 0.0, code, 0.0)
    for half, (start, size) in enumerate(((0, CUT), (CUT, MSG_COLS))):
        in_half = (within >= 8) if half else (within < 8)
        select = jnp.where(wanted == jnp.where(in_half, code, 0.0), 1.0, 0.0).astype(jnp.bfloat16)
        rows = recv[:, :, :size].reshape(shape[1], size)
        out[:, start : start + size] = dot(select, rows).astype(jnp.bfloat16)


def routed(tiles, owners, offsets, devices, capacity, tile_h, tile_w):
    tile_count, tile_size = tiles[0].shape
    vmem = pl.BlockSpec(memory_space=pltpu.VMEM)
    buffer = pltpu.VMEM((devices, MSG_ROWS, MSG_COLS), jnp.bfloat16)
    blocks = pl.pallas_call(
        functools.partial(route_kernel, capacity=capacity, tile_h=tile_h, tile_w=tile_w),
        out_shape=jax.ShapeDtypeStruct((2 * tile_count, tile_size), jnp.bfloat16),
        in_specs=[vmem] * 6,
        out_specs=vmem,
        scratch_shapes=[
            buffer,
            buffer,
            pltpu.VMEM((1, devices * MSG_ROWS), jnp.float32),
            pltpu.SemaphoreType.DMA((devices,)),
            pltpu.SemaphoreType.DMA((devices,)),
        ],
        compiler_params=pltpu.CompilerParams(
            collective_id=2, has_side_effects=True, vmem_limit_bytes=40 * 1024 * 1024
        ),
    )(
        *tiles,
        *(owner.reshape(1, tile_count) for owner in owners),
        *(offset.T for offset in offsets),
    )
    return (
        blocks.reshape(2, TY, TX, tile_h, tile_w)
        .transpose(0, 1, 3, 2, 4)
        .reshape(2, TY * tile_h, TX * tile_w)
    )


def per_device(a_tiles, a_owner, a_offset, b_tiles, b_owner, b_offset, patch_valid):
    grid_rows, grid_cols = patch_valid.shape
    tile_h = grid_rows * STRIDE // TY
    tile_w = grid_cols * STRIDE // TX
    devices = lax.axis_size("row") * lax.axis_size("col")
    capacity = 4 * a_tiles.shape[0] // (3 * devices)
    canvas = routed(
        (a_tiles, b_tiles),
        (a_owner, b_owner),
        (a_offset, b_offset),
        devices,
        capacity,
        tile_h,
        tile_w,
    )
    return measured(canvas, patch_valid)


def solution(mesh):
    in_specs = (
        P(("row", "col"), None),
        P(("row", "col")),
        P(("row", "col"), None),
        P(("row", "col"), None),
        P(("row", "col")),
        P(("row", "col"), None),
        P("row", "col"),
    )
    out_specs = (P(None, "row", "col"), P(None, "row", "col"))
    return jax.shard_map(
        per_device, mesh=mesh, in_specs=in_specs, out_specs=out_specs, check_vma=False
    )
```

```python
import functools
import math

import jax
import jax.numpy as jnp
import ml_dtypes
import numpy as np
from jax import lax
from jax.experimental import pallas as pl
from jax.experimental.pallas import tpu as pltpu
from jax.sharding import PartitionSpec as P

PATCH = 160
STRIDE = 40
TY = 12
TX = 8
SWEEPS = 3
MARGIN = 60


stiffness = 1.0
tiny = 1e-06


HALF = PATCH // 2 + 1
KPAD = 88
EDGE_R = 64
EDGE_C = 128
ROWS = 608
COLS = 896
ROW0 = EDGE_R - MARGIN
COL0 = EDGE_C - MARGIN
WIN = 208
MESH = pl.DeviceIdType.MESH


def tables():
    index = np.arange(PATCH, dtype=np.int64)
    phase = (index[:, None] * index[None, :] % PATCH).astype(np.float32) * np.float32(
        2.0 * math.pi / PATCH
    )
    cos = np.cos(phase).astype(ml_dtypes.bfloat16).astype(np.float32)
    sin = np.sin(phase).astype(ml_dtypes.bfloat16).astype(np.float32)
    sin[(index[:, None] * index[None, :]) % 80 == 0] = 0.0
    first = np.zeros((2, 416, 256), np.float32)
    for parity in range(2):
        top = 132 + 8 * parity
        first[parity, top : top + PATCH, :HALF] = cos[:, :HALF]
        first[parity, top : top + PATCH, 128 : 128 + HALF] = sin[:, :HALF]
    second = np.zeros((4 * KPAD, WIN), np.float32)
    for parity in range(2):
        left = ROW0 + STRIDE * parity
        top = 2 * KPAD * parity
        second[top : top + HALF, left : left + PATCH] = cos[:HALF]
        second[top + KPAD : top + KPAD + HALF, left : left + PATCH] = sin[:HALF]
    once = np.ones(HALF, np.float32)
    once[0] = once[-1] = 0.5
    third = np.zeros((PATCH, 2 * KPAD), np.float32)
    third[:, :HALF] = cos[:, :HALF] * once
    third[:, KPAD : KPAD + HALF] = sin[:, :HALF]
    fourth = np.zeros((256, 256), np.float32)
    fourth[:HALF, :PATCH] = cos[:HALF] * (2.0 * once)[:, None]
    fourth[128 : 128 + HALF, :PATCH] = -2.0 * sin[:HALF]
    band_rows = np.zeros((16, ROWS), np.float32)
    for i in range(12):
        band_rows[i, ROW0 + STRIDE * i : ROW0 + STRIDE * i + PATCH] = 1.0
    band_cols = np.zeros((COLS, 128), np.float32)
    for j in range(16):
        band_cols[COL0 + STRIDE * j : COL0 + STRIDE * j + PATCH, j] = 1.0
    as_bf16 = [jnp.asarray(t, jnp.bfloat16) for t in (first, second, third, fourth, band_rows)]
    return (*as_bf16, jnp.asarray(band_cols, jnp.float32))


def dot(left, right):
    return jnp.dot(left, right, preferred_element_type=jnp.float32)


def section_kernel(
    strips, valid, first, second, third, fourth, band_rows, band_cols, flow, mesh,
    images, spec, scale, parts, spectra_0, spectra_1, inverse_0, inverse_1,
    sure, mine, near, send_sem, recv_sem,
):
    row, col = lax.axis_index("row"), lax.axis_index("col")
    grid_rows, grid_cols = valid.shape
    _, strip_count, height, strip_width = strips.shape
    width = strip_count * strip_width
    near[...] = jnp.zeros(near.shape, jnp.float32)
    copies = halo_copies(images, height, width, row, col, send_sem, recv_sem)
    greet_neighbours(row, col)
    for section in range(2):
        for n in range(strip_count):
            left = EDGE_C + n * strip_width
            images[section, EDGE_R : EDGE_R + height, left : left + strip_width] = strips[section, n]
    await_neighbours(row, col)
    start(row, col, copies)

    def first_part(section, top, count, columns):
        for j in columns:
            left = (COL0 + STRIDE * j) // 128 * 128
            inside = COL0 + STRIDE * j - left
            width = 256 if inside + PATCH <= 256 else 384
            parity = inside // 8 % 2
            base = 132 + 8 * parity - inside
            strip = images[section, top : top + count, left : left + width]
            spec[section, top : top + count, 256 * j : 256 * (j + 1)] = dot(
                strip, first[parity, base : base + width, :]
            ).astype(jnp.bfloat16)

    half = height // 2
    inner = [j for j in range(2, grid_cols - 2)]
    outer = [j for j in range(grid_cols) if j not in inner]

    def first_inner(section, carry):
        for top in (EDGE_R, EDGE_R + half):
            first_part(section, top, half, inner)
        return carry

    def first_outer(section, carry):
        for top in (EDGE_R, EDGE_R + half):
            first_part(section, top, half, outer)
        for top in (0, EDGE_R + height):
            first_part(section, top, EDGE_R, range(grid_cols))
        return carry

    lax.fori_loop(0, 2, first_inner, 0)
    finish(row, col, copies)
    lax.fori_loop(0, 2, first_outer, 0)

    norms = []
    for section in range(2):
        values = images[section].astype(jnp.float32)
        squares = values * values
        high = squares.astype(jnp.bfloat16)
        low = (squares - high.astype(jnp.float32)).astype(jnp.bfloat16)
        by_rows = dot(band_rows[...], high) + dot(band_rows[...], low)
        total = jnp.dot(
            by_rows,
            band_cols[...],
            preferred_element_type=jnp.float32,
            precision=lax.Precision.HIGHEST,
        )
        norms.append(PATCH * jnp.sqrt(total / (PATCH * PATCH) + tiny))
    inv_norms = 1.0 / (norms[0] * norms[1])
    scale[...] = (inv_norms * (1.0 / (PATCH * PATCH))) * (inv_norms * (1.0 / (PATCH * PATCH)))

    lane = lax.broadcasted_iota(jnp.int32, (8, 256), 1)
    sublane = lax.broadcasted_iota(jnp.int32, (8, 256), 0)
    unit = 16.0 / PATCH
    shift_x = jnp.where(lane < PATCH // 2, lane, lane - PATCH).astype(jnp.float32) * unit
    shift_x = jnp.where(lane < PATCH, shift_x, 0.0)
    shift_y = (sublane + PATCH // 2).astype(jnp.float32) * unit

    pairs = grid_rows // 2 * grid_cols

    def forward(t, spectra):
        t = jnp.minimum(t, pairs - 1)
        top = pl.multiple_of(t // grid_cols * (2 * STRIDE), 16)
        left = pl.multiple_of(t % grid_cols * 256, 256)
        for section in range(2):
            spectra[section] = dot(second[...], spec[section, pl.ds(top, WIN), pl.ds(left, 256)])

    def combos(spectra, section, parity):
        top = 2 * KPAD * parity
        a = spectra[section, top : top + KPAD, :128]
        e = spectra[section, top : top + KPAD, 128:]
        d = spectra[section, top + KPAD : top + 2 * KPAD, :128]
        b = spectra[section, top + KPAD : top + 2 * KPAD, 128:]
        return a - b, d + e, a + b, e - d

    def crossed(spectra, inverse):
        for parity in range(2):
            ra, ia, ra_m, ia_m = combos(spectra, 0, parity)
            rb, ib, rb_m, ib_m = combos(spectra, 1, parity)
            real, imag = ra * rb + ia * ib, ia * rb - ra * ib
            real_m, imag_m = ra_m * rb_m + ia_m * ib_m, ia_m * rb_m - ra_m * ib_m
            upper = jnp.concatenate([real + real_m, imag + imag_m], axis=1)
            lower = jnp.concatenate([imag_m - imag, real - real_m], axis=1)
            cross = jnp.concatenate([upper, lower], axis=0).astype(jnp.bfloat16)
            inverse[PATCH * parity : PATCH * (parity + 1)] = dot(third[...], cross).astype(
                jnp.bfloat16
            )

    def summed(t, inverse):
        corr = dot(inverse[...], fourth[...])
        for parity in range(2):
            sum_0 = jnp.zeros((8, 256), jnp.float32)
            sum_1 = jnp.zeros((8, 256), jnp.float32)
            for block in range(PATCH // 8):
                top = PATCH * parity + (block * 8 + PATCH // 2) % PATCH
                piece = corr[top : top + 8]
                sum_0 = sum_0 + piece * piece
                sum_1 = sum_1 + sum_0
            moments = (sum_0, shift_y * sum_0 - (8.0 * unit) * sum_1, shift_x * sum_0)
            for c, part in enumerate(moments):
                part = part[:, :128] + part[:, 128:]
                parts[c, parity, pl.ds(t + 1, 1), :] = jnp.sum(part, axis=0, keepdims=True)

    inverse_1[...] = jnp.zeros(inverse_1.shape, jnp.bfloat16)
    forward(0, spectra_0)

    def step(u, carry):
        t = 2 * u
        summed(t - 1, inverse_1)
        crossed(spectra_0, inverse_0)
        forward(t + 1, spectra_1)
        summed(t, inverse_0)
        crossed(spectra_1, inverse_1)
        forward(t + 2, spectra_0)
        return carry

    lax.fori_loop(0, pairs // 2, step, 0)
    summed(pairs - 1, inverse_1)

    ones = jnp.ones((8, 128), jnp.float32)
    for i in range(grid_rows):
        first_pair = i // 2 * grid_cols + 1
        sums = [
            lax.dot_general(
                ones,
                parts[c, i % 2, first_pair : first_pair + grid_cols, :],
                (((1,), (1,)), ((), ())),
                preferred_element_type=jnp.float32,
                precision=lax.Precision.HIGHEST,
            )[:1]
            * scale[i : i + 1, :grid_cols]
            for c in range(3)
        ]
        below = 1.0 + sums[0]
        sure[i : i + 1, :] = sums[0] / below
        flow[0, i : i + 1, :] = sums[1] / below
        flow[1, i : i + 1, :] = sums[2] / below
    relax(flow, sure, valid, mesh, mine, near, send_sem, recv_sem)


def measured(strips, valid):
    grid_rows, grid_cols = valid.shape
    vmem = pl.BlockSpec(memory_space=pltpu.VMEM)
    field = jax.ShapeDtypeStruct((2, grid_rows, grid_cols), jnp.float32)
    return pl.pallas_call(
        section_kernel,
        out_shape=(field, field),
        in_specs=[vmem] * 8,
        out_specs=(vmem, vmem),
        scratch_shapes=[
            pltpu.VMEM((2, ROWS, COLS), jnp.bfloat16),
            pltpu.VMEM((2, ROWS, 256 * grid_cols), jnp.bfloat16),
            pltpu.VMEM((16, 128), jnp.float32),
            pltpu.VMEM((3, 2, grid_rows // 2 * grid_cols + 8, 128), jnp.float32),
            pltpu.VMEM((2, 4 * KPAD, 256), jnp.float32),
            pltpu.VMEM((2, 4 * KPAD, 256), jnp.float32),
            pltpu.VMEM((2 * PATCH, 256), jnp.bfloat16),
            pltpu.VMEM((2 * PATCH, 256), jnp.bfloat16),
            pltpu.VMEM((grid_rows, grid_cols), jnp.float32),
            pltpu.VMEM((3, 24, 128), jnp.float32),
            pltpu.VMEM((8, 3, 24, 128), jnp.float32),
            pltpu.SemaphoreType.DMA((16,)),
            pltpu.SemaphoreType.DMA((16,)),
        ],
        compiler_params=pltpu.CompilerParams(
            collective_id=0, has_side_effects=True, vmem_limit_bytes=48 * 1024 * 1024
        ),
    )(strips, valid, *tables())


DIRECTIONS = [(dr, dc) for dr in (-1, 0, 1) for dc in (-1, 0, 1) if (dr, dc) != (0, 0)]


def exists(row, col):
    return (
        (row >= 0)
        & (row < lax.axis_size("row"))
        & (col >= 0)
        & (col < lax.axis_size("col"))
    )


def greet_neighbours(row, col):
    barrier = pltpu.get_barrier_semaphore()
    for dr, dc in DIRECTIONS:

        @pl.when(exists(row + dr, col + dc))
        def _(dr=dr, dc=dc):
            pl.semaphore_signal(
                barrier, inc=1, device_id=(row + dr, col + dc), device_id_type=MESH
            )


def await_neighbours(row, col):
    def along(index, axis):
        return 1 + jnp.where(index > 0, 1, 0) + jnp.where(index < lax.axis_size(axis) - 1, 1, 0)

    pl.semaphore_wait(pltpu.get_barrier_semaphore(), along(row, "row") * along(col, "col") - 1)


def start(row, col, copies):
    for (dr, dc), copy in zip(DIRECTIONS, copies):

        @pl.when(exists(row + dr, col + dc))
        def _(copy=copy):
            copy.start()


def finish(row, col, copies):
    for (dr, dc), copy in zip(DIRECTIONS, copies):

        @pl.when(exists(row + dr, col + dc))
        def _(copy=copy):
            copy.wait_send()

        @pl.when(exists(row - dr, col - dc))
        def _(copy=copy):
            copy.wait_recv()


def halo_copies(image, height, width, row, col, send_sem, recv_sem):
    image[:, :EDGE_R, :] = jnp.zeros((2, EDGE_R, COLS), jnp.bfloat16)
    image[:, EDGE_R + height :, :] = jnp.zeros((2, EDGE_R, COLS), jnp.bfloat16)
    side = jnp.zeros((2, height, EDGE_C), jnp.bfloat16)
    image[:, EDGE_R : EDGE_R + height, :EDGE_C] = side
    image[:, EDGE_R : EDGE_R + height, EDGE_C + width :] = side
    rows = {
        -1: (slice(EDGE_R, 2 * EDGE_R), slice(EDGE_R + height, ROWS)),
        0: (slice(EDGE_R, EDGE_R + height), slice(EDGE_R, EDGE_R + height)),
        1: (slice(height, EDGE_R + height), slice(0, EDGE_R)),
    }
    cols = {
        -1: (slice(EDGE_C, 2 * EDGE_C), slice(EDGE_C + width, COLS)),
        0: (slice(EDGE_C, EDGE_C + width), slice(EDGE_C, EDGE_C + width)),
        1: (slice(width, EDGE_C + width), slice(0, EDGE_C)),
    }
    return [
        pltpu.make_async_remote_copy(
            src_ref=image.at[:, rows[dr][0], cols[dc][0]],
            dst_ref=image.at[:, rows[dr][1], cols[dc][1]],
            send_sem=send_sem.at[d],
            recv_sem=recv_sem.at[d],
            device_id=(row + dr, col + dc),
            device_id_type=MESH,
        )
        for d, (dr, dc) in enumerate(DIRECTIONS)
    ]


def relax(flow, sure, valid, out, mine, near, send_sem, recv_sem):
    row, col = lax.axis_index("row"), lax.axis_index("col")
    grid_rows, grid_cols = valid.shape
    mine[...] = jnp.zeros(mine.shape, jnp.float32)
    usable = valid[...].astype(jnp.float32)
    mine[0, :grid_rows, :grid_cols] = usable * sure[...]
    mine[1, :grid_rows, :grid_cols] = usable * flow[0]
    mine[2, :grid_rows, :grid_cols] = usable * flow[1]
    copies = [
        pltpu.make_async_remote_copy(
            src_ref=mine,
            dst_ref=near.at[d],
            send_sem=send_sem.at[8 + d],
            recv_sem=recv_sem.at[8 + d],
            device_id=(row + dr, col + dc),
            device_id_type=MESH,
        )
        for d, (dr, dc) in enumerate(DIRECTIONS)
    ]
    start(row, col, copies)
    finish(row, col, copies)
    shape = mine.shape[1:]
    i = lax.broadcasted_iota(jnp.int32, shape, 0)
    j = lax.broadcasted_iota(jnp.int32, shape, 1)

    def within(index, d, count):
        low = {-1: 0, 0: SWEEPS, 1: SWEEPS + count}[d]
        high = {-1: SWEEPS, 0: SWEEPS + count, 1: 2 * SWEEPS + count}[d]
        return (index >= low) & (index < high)

    def moved(block, down, right):
        if down % shape[0]:
            block = pltpu.roll(block, down % shape[0], 0)
        if right % shape[1]:
            block = pltpu.roll(block, right % shape[1], 1)
        return block

    fields = []
    for f in range(3):
        total = jnp.zeros(shape, jnp.float32)
        for dr in (-1, 0, 1):
            for dc in (-1, 0, 1):
                if (dr, dc) == (0, 0):
                    block = mine[f]
                else:
                    block = near[DIRECTIONS.index((-dr, -dc)), f]
                block = moved(block, SWEEPS + grid_rows * dr, SWEEPS + grid_cols * dc)
                here = within(i, dr, grid_rows) & within(j, dc, grid_cols)
                total = jnp.where(here, block, total)
        fields.append(total)
    strength, start_y, start_x = fields
    grid_i = row * grid_rows + i - SWEEPS
    grid_j = col * grid_cols + j - SWEEPS
    inside = (
        (grid_i >= 0)
        & (grid_i < lax.axis_size("row") * grid_rows)
        & (grid_j >= 0)
        & (grid_j < lax.axis_size("col") * grid_cols)
        & (i < grid_rows + 2 * SWEEPS)
        & (j < grid_cols + 2 * SWEEPS)
    )
    for f, initial in enumerate((start_y, start_x)):
        pull = strength * initial
        field = initial
        for _ in range(SWEEPS):
            around = moved(field, 1, 0) + moved(field, -1, 0)
            around = around + moved(field, 0, 1) + moved(field, 0, -1)
            field = (pull + stiffness * around) / (strength + 4.0 * stiffness)
            field = jnp.where(inside, field, 0.0)
        out[f] = moved(field, -SWEEPS, -SWEEPS)[:grid_rows, :grid_cols]


MSG_ROWS = 16
CUT = 1536
MSG_COLS = 1664


def route_kernel(
    a_hbm, b_hbm, a_owner_hbm, b_owner_hbm, a_offset_hbm, b_offset_hbm, out, send, recv, code_rows, send_sem, recv_sem,
    a_tiles, b_tiles, a_owner, b_owner, a_offset, b_offset, load_sem,
    *, capacity, tile_h, tile_w,
):
    loads = [
        pltpu.make_async_copy(source, target, load_sem.at[n])
        for n, (source, target) in enumerate(
            (
                (a_owner_hbm, a_owner),
                (b_owner_hbm, b_owner),
                (a_offset_hbm, a_offset),
                (b_offset_hbm, b_offset),
                (a_hbm, a_tiles),
                (b_hbm, b_tiles),
            )
        )
    ]
    for load in loads:
        load.start()
    row, col = lax.axis_index("row"), lax.axis_index("col")
    col_count = lax.axis_size("col")
    devices = lax.axis_size("row") * col_count
    me = row * col_count + col
    tile_count = a_tiles.shape[0]
    chunk = 128 // MSG_ROWS
    barrier = pltpu.get_barrier_semaphore()

    def device(k):
        target = lax.rem(me + k, devices)
        return (lax.div(target, col_count), lax.rem(target, col_count))

    def greet(k, carry):
        pl.semaphore_signal(barrier, inc=1, device_id=device(k), device_id_type=MESH)
        return carry

    lax.fori_loop(1, devices, greet, 0)

    def copy(k):
        return pltpu.make_async_remote_copy(
            src_ref=send.at[k],
            dst_ref=recv.at[k],
            send_sem=send_sem.at[k],
            recv_sem=recv_sem.at[k],
            device_id=device(k),
            device_id_type=MESH,
        )

    for load in loads[:4]:
        load.wait()
    earlier = lax.broadcasted_iota(jnp.int32, (tile_count, tile_count), 0)
    later = lax.broadcasted_iota(jnp.int32, (tile_count, tile_count), 1)
    targets, places = [], []
    for section, (owner, offset) in enumerate(((a_owner, a_offset), (b_owner, b_offset))):
        across = owner[...].astype(jnp.float32)
        down = jnp.sum(jnp.where(earlier == later, across, 0.0), axis=1, keepdims=True)
        same = (down == across) & (earlier < later)
        rank = jnp.sum(jnp.where(same, 1.0, 0.0), axis=0, keepdims=True)
        ahead = across - me.astype(jnp.float32)
        ahead = jnp.where(ahead < 0.0, ahead + devices, ahead)
        targets.append(ahead * MSG_ROWS + rank + section * capacity)
        at = offset[...].astype(jnp.float32)
        place_y = jnp.floor(at[0:1] * (1.0 / tile_h) + 0.5)
        place_x = jnp.floor(at[1:2] * (1.0 / tile_w) + 0.5)
        places.append(place_y * TX + place_x + 1.0)
    slot = lax.broadcasted_iota(jnp.int32, (128, tile_count), 0)
    for load in loads[4:]:
        load.wait()

    def fill(c, carry):
        here = (slot + c * 128).astype(jnp.float32)
        code = jnp.zeros((128, 1), jnp.float32)
        left = jnp.zeros((128, CUT), jnp.float32)
        right = jnp.zeros((128, MSG_COLS - CUT), jnp.float32)
        for tiles, target, place in zip((a_tiles, b_tiles), targets, places):
            upper = jnp.where(here == target, 1.0, 0.0)
            lower = jnp.where(here == target + 8.0, 1.0, 0.0).astype(jnp.bfloat16)
            code = code + jnp.sum(upper * place, axis=1, keepdims=True)
            left = left + dot(upper.astype(jnp.bfloat16), tiles[:, :CUT])
            left = left + dot(lower, tiles[:, CUT : 2 * CUT])
            right = right + dot(lower, tiles[:, 2 * CUT :])
        block = pl.ds(c * chunk, chunk)
        send[block, :, :CUT] = left.astype(jnp.bfloat16).reshape(chunk, MSG_ROWS, CUT)
        send[block, :, CUT:] = (
            (right + code).astype(jnp.bfloat16).reshape(chunk, MSG_ROWS, MSG_COLS - CUT)
        )

        @pl.when(c == 0)
        def _():
            pl.semaphore_wait(barrier, devices - 1)
            recv[0] = send[0]

        def push(k, carry):
            copy(k).start()
            return carry

        lax.fori_loop(jnp.maximum(c * chunk, 1), (c + 1) * chunk, push, 0)
        return carry

    lax.fori_loop(0, devices // chunk, fill, 0)

    def arrive(k, carry):
        copy(k).wait()
        return carry

    lax.fori_loop(1, devices, arrive, 0)

    from_row = lax.broadcasted_iota(jnp.int32, (128, 128), 0)
    to_lane = lax.broadcasted_iota(jnp.int32, (128, 128), 1)
    to_lane = jnp.where((to_lane & 15) >= 8, to_lane - 8, to_lane)
    for c in range(devices // chunk):
        codes = recv[c * chunk : (c + 1) * chunk, :, CUT:].reshape(128, 128).astype(jnp.float32)
        code_rows[:, 128 * c : 128 * (c + 1)] = jnp.sum(
            jnp.where(from_row == to_lane, codes[:, :1], 0.0), axis=0, keepdims=True
        )
    shape = (2 * tile_count, devices * MSG_ROWS)
    wanted = lax.broadcasted_iota(jnp.int32, shape, 0).astype(jnp.float32) + 1.0
    within = lax.broadcasted_iota(jnp.int32, (1, shape[1]), 1) & 15
    code = code_rows[...]
    code = jnp.where((within & 7) >= capacity, code + tile_count, code)
    code = jnp.where(code_rows[...] > 0.0, code, 0.0)
    for half, (start, size) in enumerate(((0, CUT), (CUT, MSG_COLS))):
        in_half = (within >= 8) if half else (within < 8)
        select = jnp.where(wanted == jnp.where(in_half, code, 0.0), 1.0, 0.0).astype(jnp.bfloat16)
        rows = recv[:, :, :size].reshape(shape[1], size)
        out[:, start : start + size] = dot(select, rows).astype(jnp.bfloat16)


def routed(tiles, owners, offsets, devices, capacity, tile_h, tile_w):
    tile_count, tile_size = tiles[0].shape
    vmem = pl.BlockSpec(memory_space=pltpu.VMEM)
    buffer = pltpu.VMEM((devices, MSG_ROWS, MSG_COLS), jnp.bfloat16)
    blocks = pl.pallas_call(
        functools.partial(route_kernel, capacity=capacity, tile_h=tile_h, tile_w=tile_w),
        out_shape=jax.ShapeDtypeStruct((2 * tile_count, tile_size), jnp.bfloat16),
        in_specs=[pl.BlockSpec(memory_space=pltpu.HBM)] * 6,
        out_specs=vmem,
        scratch_shapes=[
            buffer,
            buffer,
            pltpu.VMEM((1, devices * MSG_ROWS), jnp.float32),
            pltpu.SemaphoreType.DMA((devices,)),
            pltpu.SemaphoreType.DMA((devices,)),
            *[pltpu.VMEM((tile_count, tile_size), jnp.bfloat16)] * 2,
            *[pltpu.VMEM((1, tile_count), jnp.int32)] * 2,
            *[pltpu.VMEM((2, tile_count), jnp.int32)] * 2,
            pltpu.SemaphoreType.DMA((6,)),
        ],
        compiler_params=pltpu.CompilerParams(
            collective_id=2, has_side_effects=True, vmem_limit_bytes=63 * 1024 * 1024
        ),
    )(
        *tiles,
        *(owner.reshape(1, tile_count) for owner in owners),
        *(offset.T for offset in offsets),
    )
    return (
        blocks.reshape(2, TY, TX, tile_h, tile_w)
        .transpose(0, 2, 1, 3, 4)
        .reshape(2, TX, TY * tile_h, tile_w)
    )


def per_device(a_tiles, a_owner, a_offset, b_tiles, b_owner, b_offset, patch_valid):
    grid_rows, grid_cols = patch_valid.shape
    tile_h = grid_rows * STRIDE // TY
    tile_w = grid_cols * STRIDE // TX
    devices = lax.axis_size("row") * lax.axis_size("col")
    capacity = 4 * a_tiles.shape[0] // (3 * devices)
    strips = routed(
        (a_tiles, b_tiles),
        (a_owner, b_owner),
        (a_offset, b_offset),
        devices,
        capacity,
        tile_h,
        tile_w,
    )
    return measured(strips, patch_valid)


def solution(mesh):
    in_specs = (
        P(("row", "col"), None),
        P(("row", "col")),
        P(("row", "col"), None),
        P(("row", "col"), None),
        P(("row", "col")),
        P(("row", "col"), None),
        P("row", "col"),
    )
    out_specs = (P(None, "row", "col"), P(None, "row", "col"))
    return jax.shard_map(
        per_device, mesh=mesh, in_specs=in_specs, out_specs=out_specs, check_vma=False
    )
```

```python
import functools
import math

import jax
import jax.numpy as jnp
import ml_dtypes
import numpy as np
from jax import lax
from jax.experimental import pallas as pl
from jax.experimental.pallas import tpu as pltpu
from jax.sharding import PartitionSpec as P

PATCH = 160
STRIDE = 40
TY = 12
TX = 8
SWEEPS = 3
MARGIN = 60


stiffness = 1.0
tiny = 1e-06


HALF = PATCH // 2 + 1
KPAD = 88
EDGE_R = 64
EDGE_C = 128
ROWS = 608
COLS = 896
ROW0 = EDGE_R - MARGIN
COL0 = EDGE_C - MARGIN
WIN = 208
MESH = pl.DeviceIdType.MESH


def tables():
    index = np.arange(PATCH, dtype=np.int64)
    phase = (index[:, None] * index[None, :] % PATCH).astype(np.float32) * np.float32(
        2.0 * math.pi / PATCH
    )
    cos = np.cos(phase).astype(ml_dtypes.bfloat16).astype(np.float32)
    sin = np.sin(phase).astype(ml_dtypes.bfloat16).astype(np.float32)
    sin[(index[:, None] * index[None, :]) % 80 == 0] = 0.0
    first = np.zeros((2, 416, 256), np.float32)
    for parity in range(2):
        top = 132 + 8 * parity
        first[parity, top : top + PATCH, :HALF] = cos[:, :HALF]
        first[parity, top : top + PATCH, 128 : 128 + HALF] = sin[:, :HALF]
    second = np.zeros((4 * KPAD, WIN), np.float32)
    for parity in range(2):
        left = ROW0 + STRIDE * parity
        top = 2 * KPAD * parity
        second[top : top + HALF, left : left + PATCH] = cos[:HALF]
        second[top + KPAD : top + KPAD + HALF, left : left + PATCH] = sin[:HALF]
    once = np.ones(HALF, np.float32)
    once[0] = once[-1] = 0.5
    third = np.zeros((PATCH, 2 * KPAD), np.float32)
    third[:, :HALF] = cos[:, :HALF] * once
    third[:, KPAD : KPAD + HALF] = sin[:, :HALF]
    fourth = np.zeros((256, 256), np.float32)
    fourth[:HALF, :PATCH] = cos[:HALF] * (2.0 * once)[:, None]
    fourth[128 : 128 + HALF, :PATCH] = -2.0 * sin[:HALF]
    band_rows = np.zeros((16, ROWS), np.float32)
    for i in range(12):
        band_rows[i, ROW0 + STRIDE * i : ROW0 + STRIDE * i + PATCH] = 1.0
    band_cols = np.zeros((COLS, 128), np.float32)
    for j in range(16):
        band_cols[COL0 + STRIDE * j : COL0 + STRIDE * j + PATCH, j] = 1.0
    as_bf16 = [jnp.asarray(t, jnp.bfloat16) for t in (first, second, third, fourth, band_rows)]
    return (*as_bf16, jnp.asarray(band_cols, jnp.float32))


def dot(left, right):
    return jnp.dot(left, right, preferred_element_type=jnp.float32)


def section_kernel(
    strips, valid, first, second, third, fourth, band_rows, band_cols, flow, mesh,
    images, spec, scale, parts, spectra_0, spectra_1, inverse_0, inverse_1,
    sure, mine, near, send_sem, recv_sem,
):
    row, col = lax.axis_index("row"), lax.axis_index("col")
    grid_rows, grid_cols = valid.shape
    _, strip_count, height, strip_width = strips.shape
    width = strip_count * strip_width
    near[...] = jnp.zeros(near.shape, jnp.float32)
    copies = halo_copies(images, height, width, row, col, send_sem, recv_sem)
    greet_neighbours(row, col)
    for section in range(2):
        for n in range(strip_count):
            left = EDGE_C + n * strip_width
            images[section, EDGE_R : EDGE_R + height, left : left + strip_width] = strips[section, n]
    await_neighbours(row, col)
    start(row, col, copies)

    def first_part(section, top, count, columns):
        for j in columns:
            left = (COL0 + STRIDE * j) // 128 * 128
            inside = COL0 + STRIDE * j - left
            width = 256 if inside + PATCH <= 256 else 384
            parity = inside // 8 % 2
            base = 132 + 8 * parity - inside
            strip = images[section, top : top + count, left : left + width]
            spec[section, top : top + count, 256 * j : 256 * (j + 1)] = dot(
                strip, first[parity, base : base + width, :]
            ).astype(jnp.bfloat16)

    half = height // 2
    inner = [j for j in range(2, grid_cols - 2)]
    outer = [j for j in range(grid_cols) if j not in inner]

    def first_inner(section, carry):
        for top in (EDGE_R, EDGE_R + half):
            first_part(section, top, half, inner)
        return carry

    def first_outer(section, carry):
        for top in (EDGE_R, EDGE_R + half):
            first_part(section, top, half, outer)
        for top in (0, EDGE_R + height):
            first_part(section, top, EDGE_R, range(grid_cols))
        return carry

    lax.fori_loop(0, 2, first_inner, 0)
    finish(row, col, copies)
    lax.fori_loop(0, 2, first_outer, 0)

    norms = []
    for section in range(2):
        values = images[section].astype(jnp.float32)
        squares = values * values
        high = squares.astype(jnp.bfloat16)
        low = (squares - high.astype(jnp.float32)).astype(jnp.bfloat16)
        by_rows = dot(band_rows[...], high) + dot(band_rows[...], low)
        total = jnp.dot(
            by_rows,
            band_cols[...],
            preferred_element_type=jnp.float32,
            precision=lax.Precision.HIGHEST,
        )
        norms.append(PATCH * jnp.sqrt(total / (PATCH * PATCH) + tiny))
    inv_norms = 1.0 / (norms[0] * norms[1])
    scale[...] = (inv_norms * (1.0 / (PATCH * PATCH))) * (inv_norms * (1.0 / (PATCH * PATCH)))

    lane = lax.broadcasted_iota(jnp.int32, (8, 256), 1)
    sublane = lax.broadcasted_iota(jnp.int32, (8, 256), 0)
    unit = 16.0 / PATCH
    shift_x = jnp.where(lane < PATCH // 2, lane, lane - PATCH).astype(jnp.float32) * unit
    shift_x = jnp.where(lane < PATCH, shift_x, 0.0)
    shift_y = (sublane + PATCH // 2).astype(jnp.float32) * unit

    pairs = grid_rows // 2 * grid_cols

    def forward(t, spectra):
        t = jnp.minimum(t, pairs - 1)
        top = pl.multiple_of(t // grid_cols * (2 * STRIDE), 16)
        left = pl.multiple_of(t % grid_cols * 256, 256)
        for section in range(2):
            spectra[section] = dot(second[...], spec[section, pl.ds(top, WIN), pl.ds(left, 256)])

    def combos(spectra, section, parity):
        top = 2 * KPAD * parity
        a = spectra[section, top : top + KPAD, :128]
        e = spectra[section, top : top + KPAD, 128:]
        d = spectra[section, top + KPAD : top + 2 * KPAD, :128]
        b = spectra[section, top + KPAD : top + 2 * KPAD, 128:]
        return a - b, d + e, a + b, e - d

    def crossed(spectra, inverse):
        for parity in range(2):
            ra, ia, ra_m, ia_m = combos(spectra, 0, parity)
            rb, ib, rb_m, ib_m = combos(spectra, 1, parity)
            real, imag = ra * rb + ia * ib, ia * rb - ra * ib
            real_m, imag_m = ra_m * rb_m + ia_m * ib_m, ia_m * rb_m - ra_m * ib_m
            upper = jnp.concatenate([real + real_m, imag + imag_m], axis=1)
            lower = jnp.concatenate([imag_m - imag, real - real_m], axis=1)
            cross = jnp.concatenate([upper, lower], axis=0).astype(jnp.bfloat16)
            inverse[PATCH * parity : PATCH * (parity + 1)] = dot(third[...], cross).astype(
                jnp.bfloat16
            )

    def summed(t, inverse):
        corr = dot(inverse[...], fourth[...])
        for parity in range(2):
            sum_0 = jnp.zeros((8, 256), jnp.float32)
            sum_1 = jnp.zeros((8, 256), jnp.float32)
            for block in range(PATCH // 8):
                top = PATCH * parity + (block * 8 + PATCH // 2) % PATCH
                piece = corr[top : top + 8]
                sum_0 = sum_0 + piece * piece
                sum_1 = sum_1 + sum_0
            moments = (sum_0, shift_y * sum_0 - (8.0 * unit) * sum_1, shift_x * sum_0)
            for c, part in enumerate(moments):
                part = part[:, :128] + part[:, 128:]
                parts[c, parity, pl.ds(t + 1, 1), :] = jnp.sum(part, axis=0, keepdims=True)

    inverse_1[...] = jnp.zeros(inverse_1.shape, jnp.bfloat16)
    forward(0, spectra_0)

    def step(u, carry):
        t = 2 * u
        summed(t - 1, inverse_1)
        crossed(spectra_0, inverse_0)
        forward(t + 1, spectra_1)
        summed(t, inverse_0)
        crossed(spectra_1, inverse_1)
        forward(t + 2, spectra_0)
        return carry

    lax.fori_loop(0, pairs // 2, step, 0, unroll=2)
    summed(pairs - 1, inverse_1)

    ones = jnp.ones((8, 128), jnp.float32)
    for i in range(grid_rows):
        first_pair = i // 2 * grid_cols + 1
        sums = [
            lax.dot_general(
                ones,
                parts[c, i % 2, first_pair : first_pair + grid_cols, :],
                (((1,), (1,)), ((), ())),
                preferred_element_type=jnp.float32,
                precision=lax.Precision.HIGHEST,
            )[:1]
            * scale[i : i + 1, :grid_cols]
            for c in range(3)
        ]
        below = 1.0 + sums[0]
        sure[i : i + 1, :] = sums[0] / below
        flow[0, i : i + 1, :] = sums[1] / below
        flow[1, i : i + 1, :] = sums[2] / below
    relax(flow, sure, valid, mesh, mine, near, send_sem, recv_sem)


def measured(strips, valid):
    grid_rows, grid_cols = valid.shape
    vmem = pl.BlockSpec(memory_space=pltpu.VMEM)
    field = jax.ShapeDtypeStruct((2, grid_rows, grid_cols), jnp.float32)
    return pl.pallas_call(
        section_kernel,
        out_shape=(field, field),
        in_specs=[vmem] * 8,
        out_specs=(vmem, vmem),
        scratch_shapes=[
            pltpu.VMEM((2, ROWS, COLS), jnp.bfloat16),
            pltpu.VMEM((2, ROWS, 256 * grid_cols), jnp.bfloat16),
            pltpu.VMEM((16, 128), jnp.float32),
            pltpu.VMEM((3, 2, grid_rows // 2 * grid_cols + 8, 128), jnp.float32),
            pltpu.VMEM((2, 4 * KPAD, 256), jnp.float32),
            pltpu.VMEM((2, 4 * KPAD, 256), jnp.float32),
            pltpu.VMEM((2 * PATCH, 256), jnp.bfloat16),
            pltpu.VMEM((2 * PATCH, 256), jnp.bfloat16),
            pltpu.VMEM((grid_rows, grid_cols), jnp.float32),
            pltpu.VMEM((3, 24, 128), jnp.float32),
            pltpu.VMEM((8, 3, 24, 128), jnp.float32),
            pltpu.SemaphoreType.DMA((16,)),
            pltpu.SemaphoreType.DMA((16,)),
        ],
        compiler_params=pltpu.CompilerParams(
            collective_id=0, has_side_effects=True, vmem_limit_bytes=48 * 1024 * 1024
        ),
    )(strips, valid, *tables())


DIRECTIONS = [(dr, dc) for dr in (-1, 0, 1) for dc in (-1, 0, 1) if (dr, dc) != (0, 0)]


def exists(row, col):
    return (
        (row >= 0)
        & (row < lax.axis_size("row"))
        & (col >= 0)
        & (col < lax.axis_size("col"))
    )


def greet_neighbours(row, col):
    barrier = pltpu.get_barrier_semaphore()
    for dr, dc in DIRECTIONS:

        @pl.when(exists(row + dr, col + dc))
        def _(dr=dr, dc=dc):
            pl.semaphore_signal(
                barrier, inc=1, device_id=(row + dr, col + dc), device_id_type=MESH
            )


def await_neighbours(row, col):
    def along(index, axis):
        return 1 + jnp.where(index > 0, 1, 0) + jnp.where(index < lax.axis_size(axis) - 1, 1, 0)

    pl.semaphore_wait(pltpu.get_barrier_semaphore(), along(row, "row") * along(col, "col") - 1)


def start(row, col, copies):
    for (dr, dc), copy in zip(DIRECTIONS, copies):

        @pl.when(exists(row + dr, col + dc))
        def _(copy=copy):
            copy.start()


def finish(row, col, copies):
    for (dr, dc), copy in zip(DIRECTIONS, copies):

        @pl.when(exists(row + dr, col + dc))
        def _(copy=copy):
            copy.wait_send()

        @pl.when(exists(row - dr, col - dc))
        def _(copy=copy):
            copy.wait_recv()


def halo_copies(image, height, width, row, col, send_sem, recv_sem):
    image[:, :EDGE_R, :] = jnp.zeros((2, EDGE_R, COLS), jnp.bfloat16)
    image[:, EDGE_R + height :, :] = jnp.zeros((2, EDGE_R, COLS), jnp.bfloat16)
    side = jnp.zeros((2, height, EDGE_C), jnp.bfloat16)
    image[:, EDGE_R : EDGE_R + height, :EDGE_C] = side
    image[:, EDGE_R : EDGE_R + height, EDGE_C + width :] = side
    rows = {
        -1: (slice(EDGE_R, 2 * EDGE_R), slice(EDGE_R + height, ROWS)),
        0: (slice(EDGE_R, EDGE_R + height), slice(EDGE_R, EDGE_R + height)),
        1: (slice(height, EDGE_R + height), slice(0, EDGE_R)),
    }
    cols = {
        -1: (slice(EDGE_C, 2 * EDGE_C), slice(EDGE_C + width, COLS)),
        0: (slice(EDGE_C, EDGE_C + width), slice(EDGE_C, EDGE_C + width)),
        1: (slice(width, EDGE_C + width), slice(0, EDGE_C)),
    }
    return [
        pltpu.make_async_remote_copy(
            src_ref=image.at[:, rows[dr][0], cols[dc][0]],
            dst_ref=image.at[:, rows[dr][1], cols[dc][1]],
            send_sem=send_sem.at[d],
            recv_sem=recv_sem.at[d],
            device_id=(row + dr, col + dc),
            device_id_type=MESH,
        )
        for d, (dr, dc) in enumerate(DIRECTIONS)
    ]


def relax(flow, sure, valid, out, mine, near, send_sem, recv_sem):
    row, col = lax.axis_index("row"), lax.axis_index("col")
    grid_rows, grid_cols = valid.shape
    mine[...] = jnp.zeros(mine.shape, jnp.float32)
    usable = valid[...].astype(jnp.float32)
    mine[0, :grid_rows, :grid_cols] = usable * sure[...]
    mine[1, :grid_rows, :grid_cols] = usable * flow[0]
    mine[2, :grid_rows, :grid_cols] = usable * flow[1]
    copies = [
        pltpu.make_async_remote_copy(
            src_ref=mine,
            dst_ref=near.at[d],
            send_sem=send_sem.at[8 + d],
            recv_sem=recv_sem.at[8 + d],
            device_id=(row + dr, col + dc),
            device_id_type=MESH,
        )
        for d, (dr, dc) in enumerate(DIRECTIONS)
    ]
    start(row, col, copies)
    finish(row, col, copies)
    shape = mine.shape[1:]
    i = lax.broadcasted_iota(jnp.int32, shape, 0)
    j = lax.broadcasted_iota(jnp.int32, shape, 1)

    def within(index, d, count):
        low = {-1: 0, 0: SWEEPS, 1: SWEEPS + count}[d]
        high = {-1: SWEEPS, 0: SWEEPS + count, 1: 2 * SWEEPS + count}[d]
        return (index >= low) & (index < high)

    def moved(block, down, right):
        if down % shape[0]:
            block = pltpu.roll(block, down % shape[0], 0)
        if right % shape[1]:
            block = pltpu.roll(block, right % shape[1], 1)
        return block

    fields = []
    for f in range(3):
        total = jnp.zeros(shape, jnp.float32)
        for dr in (-1, 0, 1):
            for dc in (-1, 0, 1):
                if (dr, dc) == (0, 0):
                    block = mine[f]
                else:
                    block = near[DIRECTIONS.index((-dr, -dc)), f]
                block = moved(block, SWEEPS + grid_rows * dr, SWEEPS + grid_cols * dc)
                here = within(i, dr, grid_rows) & within(j, dc, grid_cols)
                total = jnp.where(here, block, total)
        fields.append(total)
    strength, start_y, start_x = fields
    grid_i = row * grid_rows + i - SWEEPS
    grid_j = col * grid_cols + j - SWEEPS
    inside = (
        (grid_i >= 0)
        & (grid_i < lax.axis_size("row") * grid_rows)
        & (grid_j >= 0)
        & (grid_j < lax.axis_size("col") * grid_cols)
        & (i < grid_rows + 2 * SWEEPS)
        & (j < grid_cols + 2 * SWEEPS)
    )
    for f, initial in enumerate((start_y, start_x)):
        pull = strength * initial
        field = initial
        for _ in range(SWEEPS):
            around = moved(field, 1, 0) + moved(field, -1, 0)
            around = around + moved(field, 0, 1) + moved(field, 0, -1)
            field = (pull + stiffness * around) / (strength + 4.0 * stiffness)
            field = jnp.where(inside, field, 0.0)
        out[f] = moved(field, -SWEEPS, -SWEEPS)[:grid_rows, :grid_cols]


MSG_ROWS = 16
CUT = 1536
MSG_COLS = 1664


def route_kernel(
    a_hbm, b_hbm, a_owner_hbm, b_owner_hbm, a_offset_hbm, b_offset_hbm, out, send, recv, code_rows, send_sem, recv_sem,
    a_tiles, b_tiles, a_owner, b_owner, a_offset, b_offset, load_sem,
    *, capacity, tile_h, tile_w,
):
    loads = [
        pltpu.make_async_copy(source, target, load_sem.at[n])
        for n, (source, target) in enumerate(
            (
                (a_owner_hbm, a_owner),
                (b_owner_hbm, b_owner),
                (a_offset_hbm, a_offset),
                (b_offset_hbm, b_offset),
                (a_hbm, a_tiles),
                (b_hbm, b_tiles),
            )
        )
    ]
    for load in loads:
        load.start()
    row, col = lax.axis_index("row"), lax.axis_index("col")
    col_count = lax.axis_size("col")
    devices = lax.axis_size("row") * col_count
    me = row * col_count + col
    tile_count = a_tiles.shape[0]
    chunk = 128 // MSG_ROWS
    barrier = pltpu.get_barrier_semaphore()

    def device(k):
        target = lax.rem(me + k, devices)
        return (lax.div(target, col_count), lax.rem(target, col_count))

    def greet(k, carry):
        pl.semaphore_signal(barrier, inc=1, device_id=device(k), device_id_type=MESH)
        return carry

    lax.fori_loop(1, devices, greet, 0)

    def copy(k):
        return pltpu.make_async_remote_copy(
            src_ref=send.at[k],
            dst_ref=recv.at[k],
            send_sem=send_sem.at[k],
            recv_sem=recv_sem.at[k],
            device_id=device(k),
            device_id_type=MESH,
        )

    for load in loads[:4]:
        load.wait()
    earlier = lax.broadcasted_iota(jnp.int32, (tile_count, tile_count), 0)
    later = lax.broadcasted_iota(jnp.int32, (tile_count, tile_count), 1)
    targets, places = [], []
    for section, (owner, offset) in enumerate(((a_owner, a_offset), (b_owner, b_offset))):
        across = owner[...].astype(jnp.float32)
        down = jnp.sum(jnp.where(earlier == later, across, 0.0), axis=1, keepdims=True)
        same = (down == across) & (earlier < later)
        rank = jnp.sum(jnp.where(same, 1.0, 0.0), axis=0, keepdims=True)
        ahead = across - me.astype(jnp.float32)
        ahead = jnp.where(ahead < 0.0, ahead + devices, ahead)
        targets.append(ahead * MSG_ROWS + rank + section * capacity)
        at = offset[...].astype(jnp.float32)
        place_y = jnp.floor(at[0:1] * (1.0 / tile_h) + 0.5)
        place_x = jnp.floor(at[1:2] * (1.0 / tile_w) + 0.5)
        places.append(place_y * TX + place_x + 1.0)
    slot = lax.broadcasted_iota(jnp.int32, (128, tile_count), 0)
    for load in loads[4:]:
        load.wait()

    def fill(c, carry):
        here = (slot + c * 128).astype(jnp.float32)
        code = jnp.zeros((128, 1), jnp.float32)
        left = jnp.zeros((128, CUT), jnp.float32)
        right = jnp.zeros((128, MSG_COLS - CUT), jnp.float32)
        for tiles, target, place in zip((a_tiles, b_tiles), targets, places):
            upper = jnp.where(here == target, 1.0, 0.0)
            lower = jnp.where(here == target + 8.0, 1.0, 0.0).astype(jnp.bfloat16)
            code = code + jnp.sum(upper * place, axis=1, keepdims=True)
            left = left + dot(upper.astype(jnp.bfloat16), tiles[:, :CUT])
            left = left + dot(lower, tiles[:, CUT : 2 * CUT])
            right = right + dot(lower, tiles[:, 2 * CUT :])
        block = pl.ds(c * chunk, chunk)
        send[block, :, :CUT] = left.astype(jnp.bfloat16).reshape(chunk, MSG_ROWS, CUT)
        send[block, :, CUT:] = (
            (right + code).astype(jnp.bfloat16).reshape(chunk, MSG_ROWS, MSG_COLS - CUT)
        )

        @pl.when(c == 0)
        def _():
            pl.semaphore_wait(barrier, devices - 1)
            recv[0] = send[0]

        def push(k, carry):
            copy(k).start()
            return carry

        lax.fori_loop(jnp.maximum(c * chunk, 1), (c + 1) * chunk, push, 0)
        return carry

    lax.fori_loop(0, devices // chunk, fill, 0)

    def arrive(k, carry):
        copy(k).wait()
        return carry

    lax.fori_loop(1, devices, arrive, 0)

    from_row = lax.broadcasted_iota(jnp.int32, (128, 128), 0)
    to_lane = lax.broadcasted_iota(jnp.int32, (128, 128), 1)
    to_lane = jnp.where((to_lane & 15) >= 8, to_lane - 8, to_lane)
    for c in range(devices // chunk):
        codes = recv[c * chunk : (c + 1) * chunk, :, CUT:].reshape(128, 128).astype(jnp.float32)
        code_rows[:, 128 * c : 128 * (c + 1)] = jnp.sum(
            jnp.where(from_row == to_lane, codes[:, :1], 0.0), axis=0, keepdims=True
        )
    shape = (2 * tile_count, devices * MSG_ROWS)
    wanted = lax.broadcasted_iota(jnp.int32, shape, 0).astype(jnp.float32) + 1.0
    within = lax.broadcasted_iota(jnp.int32, (1, shape[1]), 1) & 15
    code = code_rows[...]
    code = jnp.where((within & 7) >= capacity, code + tile_count, code)
    code = jnp.where(code_rows[...] > 0.0, code, 0.0)
    for half, (start, size) in enumerate(((0, CUT), (CUT, MSG_COLS))):
        in_half = (within >= 8) if half else (within < 8)
        select = jnp.where(wanted == jnp.where(in_half, code, 0.0), 1.0, 0.0).astype(jnp.bfloat16)
        rows = recv[:, :, :size].reshape(shape[1], size)
        out[:, start : start + size] = dot(select, rows).astype(jnp.bfloat16)


def routed(tiles, owners, offsets, devices, capacity, tile_h, tile_w):
    tile_count, tile_size = tiles[0].shape
    vmem = pl.BlockSpec(memory_space=pltpu.VMEM)
    buffer = pltpu.VMEM((devices, MSG_ROWS, MSG_COLS), jnp.bfloat16)
    blocks = pl.pallas_call(
        functools.partial(route_kernel, capacity=capacity, tile_h=tile_h, tile_w=tile_w),
        out_shape=jax.ShapeDtypeStruct((2 * tile_count, tile_size), jnp.bfloat16),
        in_specs=[pl.BlockSpec(memory_space=pltpu.HBM)] * 6,
        out_specs=vmem,
        scratch_shapes=[
            buffer,
            buffer,
            pltpu.VMEM((1, devices * MSG_ROWS), jnp.float32),
            pltpu.SemaphoreType.DMA((devices,)),
            pltpu.SemaphoreType.DMA((devices,)),
            *[pltpu.VMEM((tile_count, tile_size), jnp.bfloat16)] * 2,
            *[pltpu.VMEM((1, tile_count), jnp.int32)] * 2,
            *[pltpu.VMEM((2, tile_count), jnp.int32)] * 2,
            pltpu.SemaphoreType.DMA((6,)),
        ],
        compiler_params=pltpu.CompilerParams(
            collective_id=2, has_side_effects=True, vmem_limit_bytes=63 * 1024 * 1024
        ),
    )(
        *tiles,
        *(owner.reshape(1, tile_count) for owner in owners),
        *(offset.T for offset in offsets),
    )
    return (
        blocks.reshape(2, TY, TX, tile_h, tile_w)
        .transpose(0, 2, 1, 3, 4)
        .reshape(2, TX, TY * tile_h, tile_w)
    )


def per_device(a_tiles, a_owner, a_offset, b_tiles, b_owner, b_offset, patch_valid):
    grid_rows, grid_cols = patch_valid.shape
    tile_h = grid_rows * STRIDE // TY
    tile_w = grid_cols * STRIDE // TX
    devices = lax.axis_size("row") * lax.axis_size("col")
    capacity = 4 * a_tiles.shape[0] // (3 * devices)
    strips = routed(
        (a_tiles, b_tiles),
        (a_owner, b_owner),
        (a_offset, b_offset),
        devices,
        capacity,
        tile_h,
        tile_w,
    )
    return measured(strips, patch_valid)


def solution(mesh):
    in_specs = (
        P(("row", "col"), None),
        P(("row", "col")),
        P(("row", "col"), None),
        P(("row", "col"), None),
        P(("row", "col")),
        P(("row", "col"), None),
        P("row", "col"),
    )
    out_specs = (P(None, "row", "col"), P(None, "row", "col"))
    return jax.shard_map(
        per_device, mesh=mesh, in_specs=in_specs, out_specs=out_specs, check_vma=False
    )
```
